128 devices in a mesh: sp: 4 (over z_hi, core), tx: 8 (over z_lo, x), ty: 4 (over y).
Axes of the slice: x: 4, y: 4, z: 4 (z_hi: 2, z_lo: 2; z = z_hi * 2 + z_lo), core: 2. Of those that a mesh axis runs over, the one named last changes fastest.
Arguments:
- mass_fractions: float32 [8, 8, 512, 1024], P('sp', None, ('tx', 'ty')), may hold values from 0 to 1
Outputs:
- correlation: float32 [28, 8, 512, 1024], P(None, 'sp', 'tx', 'ty')
The draws below stay inside these ranges and needn't reach their ends.
All inputs are finite; a program needn't handle non-finite values.
Results may differ from the reference program's by a relative error of at most 0.00013.
Values sent between devices are 32-bit elements; how exact they have to be, the bound alone decides.
A program may use at most 64 MiB of HBM per device.

```python
import jax
import jax.numpy as jnp
from jax import lax

S = 8
NX = 512
NY = 1024
NZ = 8


def shard_levels(own_key, dims, cuts, least, high):
    def one(axis_at, shards_of):
        draws = jax.random.uniform(jax.random.fold_in(jax.random.fold_in(own_key, 6), axis_at), (shards_of,), jnp.float32, least / len(cuts), high / len(cuts))
        return jnp.repeat(jnp.exp(draws), dims[axis_at] // shards_of).reshape((-1,) + (1,) * (len(dims) - axis_at - 1))

    level = one(*cuts[0])
    for cut in cuts[1:]:
        level = level * one(*cut)
    return level


def setup_inputs(seed: int = 0) -> dict:
    key_of = jax.random.split(jax.random.key(seed), 2)
    return {
        "mass_fractions": jnp.clip(1.0 * jax.random.uniform(key_of[0], (S, NZ, NX, NY), jnp.float32) ** shard_levels(key_of[0], (S, NZ, NX, NY), ((0, 4), (2, 32)), -0.2, 0.2), 0.0, 1.0),
    }


EPS = 1e-06

def window_sum(padded, which):
    length = padded.shape[which] - 4
    running = lax.slice_in_dim(padded, 0, length, axis=which)
    for offset in range(1, 5):
        running = running + lax.slice_in_dim(padded, offset, offset + length, axis=which)
    return running

def edge_counts(anchor, length_here, extent):
    position = anchor + jnp.arange(length_here, dtype=jnp.int32)
    upper = jnp.minimum(position + 2, extent - 1)
    lower = jnp.maximum(position - 2, 0)
    return (upper - lower + 1).astype(jnp.float32)

def reference(mass_fractions):
    padded = jnp.pad(mass_fractions, ((0, 0), (2, 2), (2, 2), (2, 2)))
    counts = edge_counts(0, NZ, NZ)[:, None, None] * edge_counts(0, NX, NX)[None, :, None] * edge_counts(0, NY, NY)[None, None, :]

    def filtered(cube):
        return window_sum(window_sum(window_sum(cube, 0), 1), 2) / counts
    means = [filtered(padded[i]) for i in range(S)]
    variances = [filtered(padded[i] * padded[i]) - means[i] * means[i] for i in range(S)]
    results = []
    for i in range(S):
        for j in range(i + 1, S):
            covariance = filtered(padded[i] * padded[j]) - means[i] * means[j]
            results.append(covariance / jnp.sqrt((variances[i] + EPS) * (variances[j] + EPS)))
    return jnp.stack(results)
```

```python
import functools

import jax
import jax.numpy as jnp
from jax import lax
from jax.experimental import pallas as pl
from jax.experimental.pallas import tpu as pltpu
from jax.sharding import PartitionSpec as P

EPS = 1e-06
MESH = pl.DeviceIdType.MESH
S, NZ, NX, NY = 8, 8, 512, 1024
ROWS, COLS, BLK = 64, 256, 16
PAIRS = [(i, j) for i in range(S) for j in range(i + 1, S)]
FIELDS = [(i, None) for i in range(S)] + [(i, i) for i in range(S)] + PAIRS
NF = len(FIELDS)
ORDER = (1, 3, 2)


def kernel(
    x_hbm, o_hbm, xin, m, yh, yhb, xb, yhs, xhs, zs, zh, ov,
    ysend, yrecv, zsend, zrecv, csend, crecv, lsem, osem,
):
    sp, tx, ty = (lax.axis_index(a) for a in ("sp", "tx", "ty"))
    zhi = lax.div(sp, 2)
    core = lax.rem(sp, 2)
    zsp = lax.rem(sp + 2, 4)
    csp = sp + 1 - 2 * core
    p_here = 2 * zhi
    p_there = 2 - 2 * zhi

    barrier = pltpu.get_barrier_semaphore()

    def greet(dev):
        pl.semaphore_signal(barrier, inc=1, device_id=dev, device_id_type=MESH)

    for k in (1, 2, 3):
        greet((sp, tx, lax.rem(ty + k, 4)))
    greet((zsp, tx, ty))
    greet((csp, tx, ty))

    @pl.when(tx > 0)
    def _():
        greet((sp, tx - 1, 3))

    @pl.when(tx < 7)
    def _():
        greet((sp, tx + 1, 0))

    up = jnp.logical_and(ty == 3, tx < 7)
    down = jnp.logical_and(ty == 0, tx > 0)
    load = pltpu.make_async_copy(x_hbm, xin, lsem.at[0])
    load.start()

    for s in range(S):
        m[s, 0:2] = jnp.zeros((2, 72, COLS), jnp.float32)
        m[s, 10:12] = jnp.zeros((2, 72, COLS), jnp.float32)

    @pl.when(tx == 0)
    def _():
        xb[sp, 0] = jnp.zeros((32, COLS), jnp.float32)
        yhb[sp, 0] = jnp.zeros((8, 128), jnp.float32)

    @pl.when(tx == 7)
    def _():
        xb[sp, 1] = jnp.zeros((32, COLS), jnp.float32)
        yhb[sp, 1] = jnp.zeros((8, 128), jnp.float32)

    load.wait()
    pl.semaphore_wait(barrier, 5 + 4 * up.astype(jnp.int32) + 4 * down.astype(jnp.int32))

    def rcopy(src, dst, ss, rs, dev):
        return pltpu.make_async_remote_copy(
            src_ref=src, dst_ref=dst, send_sem=ss, recv_sem=rs, device_id=dev, device_id_type=MESH
        )

    def cols(y):
        return pl.ds(pl.multiple_of(y * COLS, COLS), COLS)

    def rows(b):
        return pl.ds(pl.multiple_of(b * BLK, BLK), BLK)

    mine = pl.ds(2 * sp, 2)
    far = pl.ds(2 * zsp, 2)
    zdev = (zsp, tx, ty)
    cdev = (csp, tx, ty)
    six = pl.ds(p_here + 2, 6)
    six_there = pl.ds(p_there + 2, 6)

    def zcopy(q, b, first=False):
        src = xin.at[:, pl.ds(p_there, 6), :, cols(ty)] if first else m.at[mine, six_there, rows(b)]
        return rcopy(src, m.at[mine, six_there, rows(b)], zsend.at[q], zrecv.at[q], zdev)

    def ccopy(q, who, b, first=False):
        src = xin.at[:, pl.ds(p_here, 6), :, cols(ty)] if first else m.at[who, six, rows(b)]
        return rcopy(src, m.at[who, six, rows(b)], csend.at[q], crecv.at[q], cdev)

    sent = []

    def go(c):
        c.start()
        sent.append(c)

    go(zcopy(0, ty, True))
    ycopies = {}
    for k in ORDER:
        y = lax.rem(ty + k, 4)
        ycopies[k] = rcopy(
            xin.at[:, :, :, cols(y)], m.at[mine, pl.ds(2, 8), rows(ty)], ysend.at[k], yrecv.at[k], (sp, tx, y)
        )
        go(ycopies[k])
    go(ccopy(0, mine, ty, True))
    own = pltpu.make_async_copy(xin.at[:, :, :, cols(ty)], m.at[mine, pl.ds(2, 8), rows(ty)], lsem.at[1])
    own.start()

    lane = lax.broadcasted_iota(jnp.int32, (BLK, 128), 1)
    for y in range(4):
        acc = jnp.zeros((BLK, 128), jnp.float32)
        for s in range(2):
            for z in range(NZ):
                base = 48 * s + 4 * (z + 2)
                zero = jnp.zeros((BLK, 128), jnp.float32)
                left = xin[s, z, :, y * COLS - 128 : y * COLS] if y > 0 else zero
                right = xin[s, z, :, y * COLS + COLS : y * COLS + COLS + 128] if y < 3 else zero
                both = pltpu.roll(jnp.where(lane >= 64, left, right), base + 2, 1)
                acc = jnp.where(jnp.logical_and(lane >= base, lane < base + 4), both, acc)
        yhs[y] = acc
    for k in ORDER:
        y = lax.rem(ty + k, 4)
        c = rcopy(yhs.at[y], yh.at[sp, rows(ty)], ysend.at[4 + k], yrecv.at[4 + k], (sp, tx, y))
        ycopies[4 + k] = c
        go(c)
    ownh = pltpu.make_async_copy(yhs.at[ty], yh.at[sp, rows(ty)], lsem.at[2])
    ownh.start()

    def pack_rows(first):
        for z in range(NZ):
            for s in range(2):
                xhs[4 * z + 2 * s : 4 * z + 2 * s + 2, :] = xin[s, z, first : first + 2, :]

    def xcopies(side, y):
        dev = (sp, tx + 1 if side == 0 else tx - 1, y)
        half = 8 if side == 0 else 0
        q = 8 + 4 * side + y
        return (
            rcopy(xhs.at[:, y * COLS : (y + 1) * COLS], xb.at[sp, side], ysend.at[q], yrecv.at[8 + side], dev),
            rcopy(yhs.at[y, half : half + 8], yhb.at[sp, side], ysend.at[8 + q], yrecv.at[10 + side], dev),
        )

    for side, cond, first in ((0, up, 14), (1, down, 0)):

        @pl.when(cond)
        def _(side=side, first=first):
            pack_rows(first)
            for y in range(4):
                for c in xcopies(side, y):
                    c.start()

    own.wait()
    ownh.wait()

    def zhcopy(q, b):
        return rcopy(yh.at[sp, rows(b)], yh.at[sp, rows(b)], zsend.at[q], zrecv.at[q], zdev)

    def chcopy(q, who, b):
        return rcopy(yh.at[who, rows(b)], yh.at[who, rows(b)], csend.at[q], crecv.at[q], cdev)

    go(zhcopy(4, ty))
    go(chcopy(4, sp, ty))
    for n, k in enumerate(ORDER):
        b = lax.rem(ty + 4 - k, 4)
        ycopies[k].wait_recv()
        go(zcopy(1 + n, b))
        go(ccopy(1 + n, mine, b))
        ycopies[4 + k].wait_recv()
        go(zhcopy(5 + n, b))
        go(chcopy(5 + n, sp, b))

    @pl.when(tx > 0)
    def _():
        for c in xcopies(0, 0):
            c.wait_recv()

    @pl.when(tx < 7)
    def _():
        for c in xcopies(1, 0):
            c.wait_recv()

    def xrows(first):
        return pl.ds(pl.multiple_of(first * 4, 8), 24)

    z_x = rcopy(xb.at[sp, :, xrows(p_there)], xb.at[sp, :, xrows(p_there)], zsend.at[8], zrecv.at[8], zdev)
    z_yb = rcopy(yhb.at[sp], yhb.at[sp], zsend.at[9], zrecv.at[9], zdev)
    go(z_x)
    go(z_yb)

    def cx(q, who):
        return rcopy(xb.at[who, :, xrows(p_here)], xb.at[who, :, xrows(p_here)], csend.at[q], crecv.at[q], cdev)

    def cyb(q, who):
        return rcopy(yhb.at[who], yhb.at[who], csend.at[q], crecv.at[q], cdev)

    go(cx(8, sp))
    go(cyb(9, sp))

    for n, k in enumerate((0,) + ORDER):
        b = lax.rem(ty + 4 - k, 4)
        zcopy(n, b).wait_recv()
        go(ccopy(10 + n, far, b))
        zhcopy(4 + n, b).wait_recv()
        go(chcopy(14 + n, zsp, b))
    z_x.wait_recv()
    go(cx(18, zsp))
    z_yb.wait_recv()
    go(cyb(19, zsp))
    for q in range(4):
        b = ty
        ccopy(q, mine, b).wait_recv()
        chcopy(4 + q, sp, b).wait_recv()
        ccopy(10 + q, mine, b).wait_recv()
        chcopy(14 + q, sp, b).wait_recv()
    for q in (8, 18):
        cx(q, sp).wait_recv()
        cyb(q + 1, sp).wait_recv()

    for i in range(S):
        for z in range(NZ):
            r = 4 * z + 2 * (i % 2)
            m[i, 2 + z, 64:66, :] = xb[i // 2, 1, r : r + 2, :]
            m[i, 2 + z, 70:72, :] = xb[i // 2, 0, r : r + 2, :]
    row8 = lax.broadcasted_iota(jnp.int32, (8, 128), 0)
    for q in range(4):
        yh[q, 64:72] = jnp.where(row8 < 4, yhb[q, 1], yhb[q, 0])

    def put(f, p, ct, rt, v):
        zs[2 * f + p, ct, pl.ds(pl.multiple_of(rt * 8 + 8, 8), 8), :] = v

        @pl.when(rt == 8)
        def _():
            zs[2 * f + p, ct, 0:8, :] = v

    def stage1(rt, _):
        tile = pl.ds(pl.multiple_of(rt * 8, 8), 8)
        for ct in range(2):
            v = [[m[i, 2 * sp + k, tile, ct * 128 : ct * 128 + 128] for k in range(6)] for i in range(S)]
            for f, (i, j) in enumerate(FIELDS):
                p = v[i] if j is None else [a * b for a, b in zip(v[i], v[j])]
                mid = (p[1] + p[2]) + (p[3] + p[4])
                zs[2 * f, ct, pl.ds(pl.multiple_of(rt * 8 + 8, 8), 8), :] = p[0] + mid
                zs[2 * f + 1, ct, pl.ds(pl.multiple_of(rt * 8 + 8, 8), 8), :] = mid + p[5]
        h = [
            pltpu.roll(yh[i // 2, tile, :], lax.rem(256 - 48 * (i % 2) - 8 * sp, 128), 1) for i in range(S)
        ]
        for f, (i, j) in enumerate(FIELDS):
            p = h[i] if j is None else h[i] * h[j]
            p1 = p + pltpu.roll(p, 124, 1)
            p2 = p1 + pltpu.roll(p1, 120, 1)
            zh[f, pl.ds(pl.multiple_of(rt * 8 + 8, 8), 8), :] = p2 + pltpu.roll(p, 112, 1)
        return 0

    lax.fori_loop(0, 9, stage1, 0)

    def wrap(f, _):
        zs[2 * f, :, 0:8, :] = zs[2 * f, :, 72:80, :]
        zs[2 * f + 1, :, 0:8, :] = zs[2 * f + 1, :, 72:80, :]
        zh[f, 0:8, :] = zh[f, 72:80, :]
        return 0

    lax.fori_loop(0, NF, wrap, 0)

    lane8 = lax.broadcasted_iota(jnp.int32, (8, 128), 1)
    lt127, ge2, lt126 = lane8 < 127, lane8 >= 2, lane8 < 126

    def span(pos, extent):
        return (jnp.minimum(pos + 2, extent - 1) - jnp.maximum(pos - 2, 0) + 1).astype(jnp.float32)

    def xsum(ref, x0):
        w = [ref[pl.ds(x0 * 8 + 6 + k, 8), :] for k in range(5)]
        return ((w[0] + w[1]) + (w[2] + w[3])) + w[4]

    def stage2(x0, _):
        out_rows = pl.ds(pl.multiple_of(x0 * 8, 8), 8)
        cx_ = span(tx * ROWS + x0 * 8 + row8, NX)
        for p in range(2):
            cz = span(2 * sp + p, NZ)
            inv = [1.0 / (cx_ * span(ty * COLS + ct * 128 + lane8, NY) * cz) for ct in range(2)]

            def box(f):
                t0, t1 = (xsum(zs.at[2 * f + p, ct], x0) for ct in range(2))
                h = pltpu.roll(xsum(zh.at[f], x0), 126 - 4 * p, 1)
                r0, r1, rh = (pltpu.roll(t, 127, 1) for t in (t0, t1, h))
                a0 = t0 + jnp.where(lt127, r0, r1)
                a1 = t1 + jnp.where(lt127, r1, rh)
                ah = h + jnp.where(lt127, rh, r0)
                r0, r1, rh = (pltpu.roll(t, 2, 1) for t in (a0, a1, ah))
                b0 = a0 + jnp.where(ge2, r0, rh)
                b1 = a1 + jnp.where(ge2, r1, r0)
                r0, r1, rh = (pltpu.roll(t, 126, 1) for t in (t0, t1, h))
                return (
                    (b0 + jnp.where(lt126, r0, r1)) * inv[0],
                    (b1 + jnp.where(lt126, r1, rh)) * inv[1],
                )

            means = [box(i) for i in range(S)]
            var = []
            for i in range(S):
                sq = box(S + i)
                var.append(tuple(sq[t] - means[i][t] * means[i][t] + EPS for t in range(2)))
            for n, (i, j) in enumerate(PAIRS):
                pr = box(2 * S + n)
                for t in range(2):
                    cov = pr[t] - means[i][t] * means[j][t]
                    ov[n, p, out_rows, t * 128 : t * 128 + 128] = cov * lax.rsqrt(var[i][t] * var[j][t])
        pltpu.make_async_copy(ov.at[:, :, out_rows], o_hbm.at[:, :, out_rows], osem).start()
        return 0

    lax.fori_loop(0, 8, stage2, 0)
    pltpu.make_async_copy(ov, o_hbm, osem).wait()

    for c in sent:
        c.wait_send()
    for side, cond in ((0, up), (1, down)):

        @pl.when(cond)
        def _(side=side):
            for y in range(4):
                for c in xcopies(side, y):
                    c.wait_send()


def shards(x):
    f32 = jnp.float32
    return pl.pallas_call(
        kernel,
        out_shape=jax.ShapeDtypeStruct((len(PAIRS), 2, ROWS, COLS), f32),
        in_specs=[pl.BlockSpec(memory_space=pl.ANY)],
        out_specs=pl.BlockSpec(memory_space=pl.ANY),
        scratch_shapes=[
            pltpu.VMEM((2, NZ, BLK, NY), f32),
            pltpu.VMEM((S, 12, 72, COLS), f32),
            pltpu.VMEM((4, 72, 128), f32),
            pltpu.VMEM((4, 2, 8, 128), f32),
            pltpu.VMEM((4, 2, 32, COLS), f32),
            pltpu.VMEM((4, BLK, 128), f32),
            pltpu.VMEM((32, NY), f32),
            pltpu.VMEM((2 * NF, 2, 80, 128), f32),
            pltpu.VMEM((NF, 80, 128), f32),
            pltpu.VMEM((len(PAIRS), 2, ROWS, COLS), f32),
            pltpu.SemaphoreType.DMA((24,)),
            pltpu.SemaphoreType.DMA((12,)),
            pltpu.SemaphoreType.DMA((10,)),
            pltpu.SemaphoreType.DMA((10,)),
            pltpu.SemaphoreType.DMA((20,)),
            pltpu.SemaphoreType.DMA((20,)),
            pltpu.SemaphoreType.DMA((3,)),
            pltpu.SemaphoreType.DMA,
        ],
        name="correlate",
        compiler_params=pltpu.CompilerParams(
            collective_id=0, has_side_effects=True, vmem_limit_bytes=48 << 20
        ),
    )(x)


def solution(mesh):
    return jax.shard_map(
        shards,
        mesh=mesh,
        in_specs=(P("sp", None, ("tx", "ty"), None),),
        out_specs=P(None, "sp", "tx", "ty"),
        check_vma=False,
    )
```

```python
import functools

import jax
import jax.numpy as jnp
from jax import lax
from jax.experimental import pallas as pl
from jax.experimental.pallas import tpu as pltpu
from jax.sharding import PartitionSpec as P

EPS = 1e-06
MESH = pl.DeviceIdType.MESH
S, NZ, NX, NY = 8, 8, 512, 1024
ROWS, COLS, BLK = 64, 256, 16
PAIRS = [(i, j) for i in range(S) for j in range(i + 1, S)]
FIELDS = [(i, None) for i in range(S)] + [(i, i) for i in range(S)] + PAIRS
NF = len(FIELDS)
ORDER = (2, 1, 3)


def kernel(
    xin, o_ref, m, stage, yh, yhb, xb, yhs, xhs, zs, zh, xs, ys, band,
    zsend, zrecv, ysend, yrecv, fsend, frecv, csend, crecv, hsend, hrecv, xsend, xrecv, lsem,
):
    sp, tx, ty = (lax.axis_index(a) for a in ("sp", "tx", "ty"))
    zhi = lax.div(sp, 2)
    core = lax.rem(sp, 2)
    zsp = lax.rem(sp + 2, 4)
    csp = sp + 1 - 2 * core
    p_here = 2 * zhi
    p_there = 2 - 2 * zhi
    after = [lax.rem(ty + k, 4) for k in range(4)]
    before = [lax.rem(ty + 4 - k, 4) for k in range(4)]
    up = jnp.logical_and(ty == 3, tx < 7)
    down = jnp.logical_and(ty == 0, tx > 0)

    barrier = pltpu.get_barrier_semaphore()

    def greet(*dev):
        pl.semaphore_signal(barrier, inc=1, device_id=dev, device_id_type=MESH)

    greet(zsp, tx, ty)
    greet(csp, tx, ty)
    for k in (1, 2, 3):
        greet(sp, tx, after[k])
        greet(zsp, tx, after[k])

    @pl.when(tx > 0)
    def _():
        greet(sp, tx - 1, 3)
        greet(zsp, tx - 1, 3)

    @pl.when(tx < 7)
    def _():
        greet(sp, tx + 1, 0)
        greet(zsp, tx + 1, 0)


    for s in range(S):
        m[s, 0:2] = jnp.zeros((2, 72, COLS), jnp.float32)
        m[s, 10:12] = jnp.zeros((2, 72, COLS), jnp.float32)

    @pl.when(tx == 0)
    def _():
        xb[sp, 0] = jnp.zeros((32, COLS), jnp.float32)
        for q in (sp, zsp):
            yhb[q, 0] = jnp.zeros((8, 128), jnp.float32)

    @pl.when(tx == 7)
    def _():
        xb[sp, 1] = jnp.zeros((32, COLS), jnp.float32)
        for q in (sp, zsp):
            yhb[q, 1] = jnp.zeros((8, 128), jnp.float32)

    r_at = lax.broadcasted_iota(jnp.int32, (COLS, COLS), 0)
    c_at = lax.broadcasted_iota(jnp.int32, (COLS, COLS), 1)
    band[...] = jnp.where(jnp.abs(r_at - c_at) <= 2, 1.0, 0.0).astype(jnp.bfloat16)

    pl.semaphore_wait(barrier, 8 + 8 * up.astype(jnp.int32) + 8 * down.astype(jnp.int32))

    def rcopy(src, dst, ss, rs, dev):
        return pltpu.make_async_remote_copy(
            src_ref=src, dst_ref=dst, send_sem=ss, recv_sem=rs, device_id=dev, device_id_type=MESH
        )

    def cols(y):
        return pl.ds(pl.multiple_of(y * COLS, COLS), COLS)

    def rows(b):
        return pl.ds(pl.multiple_of(b * BLK, BLK), BLK)

    zdev = (zsp, tx, ty)
    cdev = (csp, tx, ty)
    six = pl.ds(p_here + 2, 6)
    six_there = pl.ds(p_there + 2, 6)
    sent = []

    def go(c):
        c.start()
        sent.append(c)

    def zcopy(k, s):
        src = xin.at[s, pl.ds(p_there, 6), :, cols(after[k])]
        dst = stage.at[k - 1, s] if k else m.at[2 * sp + s, six_there, rows(ty)]
        return rcopy(src, dst, zsend.at[2 * k + s], zrecv.at[2 * k + s], zdev)

    def ycopy(k):
        return rcopy(
            xin.at[:, pl.ds(p_here, 6), :, cols(after[k])],
            m.at[pl.ds(2 * sp, 2), six, rows(ty)], ysend.at[k], yrecv.at[k], (sp, tx, after[k]),
        )

    def fcopy(k, s):
        return rcopy(
            stage.at[k - 1, s], m.at[2 * zsp + s, six, rows(ty)],
            fsend.at[2 * k + s], frecv.at[2 * k + s], (sp, tx, after[k]),
        )

    def ccopy(k):
        if k == 0:
            src = xin.at[:, pl.ds(p_here, 6), :, cols(ty)]
        else:
            src = m.at[pl.ds(2 * sp, 2), six, rows(before[k])]
        return rcopy(
            src, m.at[pl.ds(2 * sp, 2), six, rows(before[k])], csend.at[k], crecv.at[k], cdev
        )

    def cfcopy(k, s):
        ref = m.at[2 * zsp + s, six, rows(before[k])]
        return rcopy(ref, ref, csend.at[4 + 2 * k + s], crecv.at[4 + 2 * k + s], cdev)

    PIECES = ((2, 0), (2, 1), (1, 0), (3, 0), (1, 1), (3, 1), (0, 0), (0, 1))
    for k, s in PIECES:
        go(zcopy(k, s))
    for k in ORDER:
        go(ycopy(k))
    go(ccopy(0))
    own = pltpu.make_async_copy(
        xin.at[:, pl.ds(p_here, 6), :, cols(ty)], m.at[pl.ds(2 * sp, 2), six, rows(ty)], lsem.at[1]
    )
    own.start()

    lane = lax.broadcasted_iota(jnp.int32, (BLK, 128), 1)
    for y in range(4):
        acc = jnp.zeros((BLK, 128), jnp.float32)
        for s in range(2):
            for z in range(NZ):
                base = 48 * s + 4 * (z + 2)
                zero = jnp.zeros((BLK, 128), jnp.float32)
                left = xin[s, z, :, y * COLS - 128 : y * COLS] if y > 0 else zero
                right = xin[s, z, :, y * COLS + COLS : y * COLS + COLS + 128] if y < 3 else zero
                right = pltpu.roll(right, base, 1)
                left = pltpu.roll(left, (base + 4) % 128, 1)
                acc = jnp.where(jnp.logical_and(lane >= base, lane < base + 2), right, acc)
                acc = jnp.where(jnp.logical_and(lane >= base + 2, lane < base + 4), left, acc)
        yhs[y] = acc

    def hcopy(k, there):
        dst_sp = zsp if there else sp
        q = 4 * there + k
        return rcopy(
            yhs.at[after[k]], yh.at[sp, rows(ty)], hsend.at[q], hrecv.at[q], (dst_sp, tx, after[k])
        )

    for k in (1, 2, 3):
        go(hcopy(k, 0))
    for k in range(4):
        go(hcopy(k, 1))
    ownh = pltpu.make_async_copy(yhs.at[ty], yh.at[sp, rows(ty)], lsem.at[2])
    ownh.start()

    def pack_rows(first):
        for z in range(NZ):
            for s in range(2):
                xhs[4 * z + 2 * s : 4 * z + 2 * s + 2, :] = xin[s, z, first : first + 2, :]

    def xrows(first):
        return pl.ds(pl.multiple_of(first * 4, 8), 24)

    def xcopies(side, y):
        tx_to = tx + 1 if side == 0 else tx - 1
        half = 8 if side == 0 else 0
        q = 3 * (4 * side + y)
        tile = yhs.at[y, half : half + 8]
        return (
            rcopy(
                xhs.at[:, y * COLS : (y + 1) * COLS], xb.at[sp, side],
                xsend.at[q], xrecv.at[3 * side], (sp, tx_to, y),
            ),
            rcopy(tile, yhb.at[sp, side], xsend.at[q + 1], xrecv.at[3 * side + 1], (sp, tx_to, y)),
            rcopy(tile, yhb.at[sp, side], xsend.at[q + 2], xrecv.at[3 * side + 2], (zsp, tx_to, y)),
        )

    for side, cond, first in ((0, up, 14), (1, down, 0)):

        @pl.when(cond)
        def _(side=side, first=first):
            pack_rows(first)
            for y in range(4):
                for c in xcopies(side, y):
                    c.start()

    own.wait()
    ownh.wait()

    def xz():
        ref = xb.at[sp, :, xrows(p_there)]
        return rcopy(ref, ref, hsend.at[8], hrecv.at[8], zdev)

    def xc(q, who):
        ref = xb.at[who, :, xrows(p_here)]
        return rcopy(ref, ref, hsend.at[9 + q], hrecv.at[9 + q], cdev)

    def yc(q, who):
        ref = yh.at[who, 0:64]
        return rcopy(ref, ref, hsend.at[11 + q], hrecv.at[11 + q], cdev)

    def bc(q, who):
        return rcopy(yhb.at[who], yhb.at[who], hsend.at[13 + q], hrecv.at[13 + q], cdev)

    def pass_z(k, s):
        zcopy(k, s).wait_recv()
        if k:
            go(fcopy(k, s))
        else:
            go(cfcopy(k, s))

    for side, cond in ((0, tx > 0), (1, tx < 7)):

        @pl.when(cond)
        def _(side=side):
            for c in xcopies(side, 0):
                c.wait_recv()

    go(xz())
    go(xc(0, sp))
    go(bc(0, sp))
    go(bc(1, zsp))
    pass_z(2, 0)
    for k in (1, 3):
        ycopy(k).wait_recv()
        go(ccopy(k))
    pass_z(2, 1)
    for k in (1, 2, 3):
        hcopy(k, 0).wait_recv()
    for k in range(4):
        hcopy(k, 1).wait_recv()
    go(yc(0, sp))
    go(yc(1, zsp))
    pass_z(1, 0)
    ycopy(2).wait_recv()
    go(ccopy(2))
    pass_z(3, 0)
    pass_z(1, 1)
    pass_z(3, 1)
    xz().wait_recv()
    go(xc(1, zsp))
    for k, s in PIECES[:-2]:
        fcopy(k, s).wait_recv()
        go(cfcopy(k, s))
    pass_z(0, 0)
    pass_z(0, 1)

    for k in range(4):
        ccopy(k).wait_recv()
        for s in range(2):
            cfcopy(k, s).wait_recv()
    for q in range(2):
        xc(q, sp).wait_recv()
        yc(q, sp).wait_recv()
        bc(q, sp).wait_recv()
    for i in range(S):
        for z in range(NZ):
            r = 4 * z + 2 * (i % 2)
            m[i, 2 + z, 64:66, :] = xb[i // 2, 1, r : r + 2, :]
            m[i, 2 + z, 70:72, :] = xb[i // 2, 0, r : r + 2, :]
    row8 = lax.broadcasted_iota(jnp.int32, (8, 128), 0)
    lane8 = lax.broadcasted_iota(jnp.int32, (8, 128), 1)
    for q in range(4):
        yh[q, 64:72] = jnp.where(row8 < 4, yhb[q, 1], yhb[q, 0])

    def stage1(rt, _):
        tile = pl.ds(pl.multiple_of(rt * 8, 8), 8)
        dst = pl.ds(pl.multiple_of(rt * 8 + 8, 8), 8)
        for ct in range(2):
            v = [[m[i, 2 * sp + k, tile, ct * 128 : ct * 128 + 128] for k in range(6)] for i in range(S)]
            for f, (i, j) in enumerate(FIELDS):
                p = v[i] if j is None else [a * b for a, b in zip(v[i], v[j])]
                mid = (p[1] + p[2]) + (p[3] + p[4])
                zs[2 * f, ct, dst, :] = p[0] + mid
                zs[2 * f + 1, ct, dst, :] = mid + p[5]
        h = [
            pltpu.roll(yh[i // 2, tile, :], lax.rem(256 - 48 * (i % 2) - 8 * sp, 128), 1) for i in range(S)
        ]
        l4 = lax.rem(lane8, 4)
        for f, (i, j) in enumerate(FIELDS):
            p = h[i] if j is None else h[i] * h[j]
            p1 = p + pltpu.roll(p, 124, 1)
            p2 = p1 + pltpu.roll(p1, 120, 1)
            q = p2 + pltpu.roll(p, 112, 1)
            zh[f, dst, :] = (
                q
                + jnp.where(l4 == 1, pltpu.roll(q, 1, 1), 0.0)
                + jnp.where(l4 == 2, pltpu.roll(q, 127, 1), 0.0)
            )
        return 0

    lax.fori_loop(0, 9, stage1, 0)

    def wrap(f, _):
        zs[2 * f, :, 0:8, :] = zs[2 * f, :, 72:80, :]
        zs[2 * f + 1, :, 0:8, :] = zs[2 * f + 1, :, 72:80, :]
        zh[f, 0:8, :] = zh[f, 72:80, :]
        return 0

    lax.fori_loop(0, NF, wrap, 0)

    def span(pos, extent):
        return (jnp.minimum(pos + 2, extent - 1) - jnp.maximum(pos - 2, 0) + 1).astype(jnp.float32)

    def xsum(ref, x0):
        w = [ref[pl.ds(x0 * 8 + 6 + k, 8), :] for k in range(5)]
        return ((w[0] + w[1]) + (w[2] + w[3])) + w[4]

    def stage2(x0, _):
        out_rows = pl.ds(pl.multiple_of(x0 * 8, 8), 8)
        for g in range(2 * NF):
            for ct in range(2):
                xs[g * 8 : g * 8 + 8, ct * 128 : ct * 128 + 128] = xsum(zs.at[g, ct], x0)
        v = xs[...]
        hi = v.astype(jnp.bfloat16)
        rest = v - hi.astype(jnp.float32)
        mid = rest.astype(jnp.bfloat16)
        low = (rest - mid.astype(jnp.float32)).astype(jnp.bfloat16)
        hi, mid, low = (
            jnp.dot(t, band[...], preferred_element_type=jnp.float32) for t in (hi, mid, low)
        )
        ys[...] = hi + (mid + low)
        hx = [xsum(zh.at[f], x0) for f in range(NF)]
        cx_ = span(tx * ROWS + x0 * 8 + row8, NX)
        for p in range(2):
            cz = span(2 * sp + p, NZ)
            inv = [1.0 / (cx_ * span(ty * COLS + ct * 128 + lane8, NY) * cz) for ct in range(2)]

            def box(f):
                g = 8 * (2 * f + p)
                c = pltpu.roll(hx[f], 126 - 4 * p, 1)
                return (
                    (ys[g : g + 8, 0:128] + jnp.where(lane8 < 2, c, 0.0)) * inv[0],
                    (ys[g : g + 8, 128:256] + jnp.where(lane8 >= 126, c, 0.0)) * inv[1],
                )

            means = [box(i) for i in range(S)]
            var = []
            for i in range(S):
                sq = box(S + i)
                var.append(tuple(sq[t] - means[i][t] * means[i][t] + EPS for t in range(2)))
            for n, (i, j) in enumerate(PAIRS):
                pr = box(2 * S + n)
                for t in range(2):
                    cov = pr[t] - means[i][t] * means[j][t]
                    o_ref[n, p, out_rows, t * 128 : t * 128 + 128] = cov * lax.rsqrt(var[i][t] * var[j][t])
        return 0

    lax.fori_loop(0, 8, stage2, 0)
    for c in sent:
        c.wait_send()
    for side, cond in ((0, up), (1, down)):

        @pl.when(cond)
        def _(side=side):
            for y in range(4):
                for c in xcopies(side, y):
                    c.wait_send()


def shards(x):
    f32 = jnp.float32
    return pl.pallas_call(
        kernel,
        out_shape=jax.ShapeDtypeStruct((len(PAIRS), 2, ROWS, COLS), f32),
        in_specs=[pl.BlockSpec(memory_space=pltpu.VMEM)],
        out_specs=pl.BlockSpec(memory_space=pltpu.VMEM),
        scratch_shapes=[
            pltpu.VMEM((S, 12, 72, COLS), f32),
            pltpu.VMEM((3, 2, 6, BLK, COLS), f32),
            pltpu.VMEM((4, 72, 128), f32),
            pltpu.VMEM((4, 2, 8, 128), f32),
            pltpu.VMEM((4, 2, 32, COLS), f32),
            pltpu.VMEM((4, BLK, 128), f32),
            pltpu.VMEM((32, NY), f32),
            pltpu.VMEM((2 * NF, 2, 80, 128), f32),
            pltpu.VMEM((NF, 80, 128), f32),
            pltpu.VMEM((16 * NF, COLS), f32),
            pltpu.VMEM((16 * NF, COLS), f32),
            pltpu.VMEM((COLS, COLS), jnp.bfloat16),
        ]
        + [pltpu.SemaphoreType.DMA((n,)) for n in (8, 8, 4, 4, 8, 8, 12, 12, 15, 15, 24, 6, 3)],
        name="correlate",
        compiler_params=pltpu.CompilerParams(
            collective_id=0, has_side_effects=True, vmem_limit_bytes=48 << 20
        ),
    )(x)


def solution(mesh):
    return jax.shard_map(
        shards,
        mesh=mesh,
        in_specs=(P("sp", None, ("tx", "ty"), None),),
        out_specs=P(None, "sp", "tx", "ty"),
        check_vma=False,
    )
```

```python
import functools

import jax
import jax.numpy as jnp
from jax import lax
from jax.experimental import pallas as pl
from jax.experimental.pallas import tpu as pltpu
from jax.sharding import PartitionSpec as P

EPS = 1e-06
MESH = pl.DeviceIdType.MESH
S, NZ, NX, NY = 8, 8, 512, 1024
ROWS, COLS, BLK = 64, 256, 16
PAIRS = [(i, j) for i in range(S) for j in range(i + 1, S)]
FIELDS = [(i, None) for i in range(S)] + [(i, i) for i in range(S)] + PAIRS
NF = len(FIELDS)
Y_ORDER = ((1, 1), (3, 0), (1, 0), (3, 1), (2, 0), (2, 1))
UNITS = ((0, 0), (0, 1)) + Y_ORDER


def kernel(
    xin, o_ref, m, yh, xb, yhs, xhs, zs, zh, xs, ys, hs, hy, band, hband,
    ysend, yrecv, esend, erecv, zsend, zrecv, csend, crecv, hsend, hrecv, xsend, xrecv, lsem,
):
    sp, tx, ty = (lax.axis_index(a) for a in ("sp", "tx", "ty"))
    zhi = lax.div(sp, 2)
    core = lax.rem(sp, 2)
    zsp = lax.rem(sp + 2, 4)
    csp = sp + 1 - 2 * core
    p_here = 2 * zhi
    p_there = 2 - 2 * zhi
    p_extra = 6 * zhi

    def after(k):
        return lax.rem(ty + k, 4)

    def before(k):
        return lax.rem(ty + 4 - k, 4)

    up = jnp.logical_and(ty == 3, tx < 7)
    down = jnp.logical_and(ty == 0, tx > 0)

    barrier = pltpu.get_barrier_semaphore()

    def greet(*dev):
        pl.semaphore_signal(barrier, inc=1, device_id=dev, device_id_type=MESH)

    greet(zsp, tx, ty)
    greet(csp, tx, ty)
    for k in (2, 1, 3):
        greet(sp, tx, after(k))

    @pl.when(tx > 0)
    def _():
        greet(sp, tx - 1, 3)

    @pl.when(tx < 7)
    def _():
        greet(sp, tx + 1, 0)

    for s in range(S):
        m[s, 0:2] = jnp.zeros((2, 72, COLS), jnp.float32)
        m[s, 10:12] = jnp.zeros((2, 72, COLS), jnp.float32)

    @pl.when(tx == 0)
    def _():
        xb[sp, 0] = jnp.zeros((40, COLS), jnp.float32)

    @pl.when(tx == 7)
    def _():
        xb[sp, 1] = jnp.zeros((40, COLS), jnp.float32)

    r_at = lax.broadcasted_iota(jnp.int32, (COLS, COLS), 0)
    c_at = lax.broadcasted_iota(jnp.int32, (COLS, COLS), 1)
    band[...] = jnp.where(jnp.abs(r_at - c_at) <= 2, 1.0, 0.0).astype(jnp.bfloat16)

    r_at = lax.broadcasted_iota(jnp.int32, (128, COLS), 0)
    c_at = lax.broadcasted_iota(jnp.int32, (128, COLS), 1)
    plane, kind, first, col = lax.div(r_at, 4), lax.rem(r_at, 4), lax.div(c_at, 128), lax.rem(c_at, 128)
    ends = (
        ((kind == 0) & (col >= 126))
        | ((kind == 1) & (col == 127))
        | ((kind == 2) & (col == 0))
        | ((kind == 3) & (col <= 1))
    )
    hband[...] = jnp.where(
        ends & (plane >= first) & (plane <= first + 4), 1.0, 0.0
    ).astype(jnp.bfloat16)

    lane = lax.broadcasted_iota(jnp.int32, (BLK, 128), 1)
    for y in range(4):
        acc = jnp.zeros((BLK, 128), jnp.float32)
        for s in range(2):
            for z in range(NZ):
                base = 48 * s + 4 * (z + 2)
                zero = jnp.zeros((BLK, 128), jnp.float32)
                left = xin[s, z, :, y * COLS - 128 : y * COLS] if y > 0 else zero
                right = xin[s, z, :, y * COLS + COLS : y * COLS + COLS + 128] if y < 3 else zero
                right = pltpu.roll(right, base, 1)
                left = pltpu.roll(left, (base + 4) % 128, 1)
                acc = jnp.where(jnp.logical_and(lane >= base, lane < base + 2), right, acc)
                acc = jnp.where(jnp.logical_and(lane >= base + 2, lane < base + 4), left, acc)
        yhs[y] = acc

    def pack_rows(first, half):
        for y in range(4):
            for z in range(NZ):
                for s in range(2):
                    r = 4 * z + 2 * s + (8 if z >= 4 else 0)
                    xhs[y, r : r + 2, :] = xin[s, z, first : first + 2, y * COLS : (y + 1) * COLS]
            xhs[y, 16:24, 0:128] = yhs[y, half : half + 8]
            xhs[y, 16:24, 128:256] = jnp.zeros((8, 128), jnp.float32)

    @pl.when(up)
    def _():
        pack_rows(14, 8)

    @pl.when(down)
    def _():
        pack_rows(0, 0)

    pl.semaphore_wait(barrier, 5 + 4 * up.astype(jnp.int32) + 4 * down.astype(jnp.int32))

    def rcopy(src, dst, ss, rs, dev):
        return pltpu.make_async_remote_copy(
            src_ref=src, dst_ref=dst, send_sem=ss, recv_sem=rs, device_id=dev, device_id_type=MESH
        )

    def cols(y):
        return pl.ds(pl.multiple_of(y * COLS, COLS), COLS)

    def rows(b):
        return pl.ds(pl.multiple_of(b * BLK, BLK), BLK)

    def tile_of(b, t):
        return pl.ds(pl.multiple_of(b * BLK + 8 * t, 8), 8)

    zdev = (zsp, tx, ty)
    cdev = (csp, tx, ty)
    mine = pl.ds(2 * sp, 2)
    far = pl.ds(2 * zsp, 2)
    six = pl.ds(p_here + 2, 6)
    six_there = pl.ds(p_there + 2, 6)

    def ycopy(k, t):
        return rcopy(
            xin.at[:, pl.ds(p_there, 6), 8 * t : 8 * t + 8, cols(after(k))],
            m.at[mine, six_there, tile_of(ty, t)],
            ysend.at[2 * k + t], yrecv.at[2 * k + t], (sp, tx, after(k)),
        )

    def ecopy(k):
        return rcopy(
            xin.at[:, pl.ds(p_extra, 2), :, cols(after(k))],
            m.at[mine, pl.ds(p_extra + 2, 2), rows(ty)],
            esend.at[k], erecv.at[k], (sp, tx, after(k)),
        )

    def zcopy(k, t, first=False):
        dst = m.at[mine, six_there, tile_of(before(k), t)]
        src = xin.at[:, pl.ds(p_there, 6), 8 * t : 8 * t + 8, cols(ty)] if first else dst
        return rcopy(src, dst, zsend.at[2 * k + t], zrecv.at[2 * k + t], zdev)

    def ccopy(k, t, first=False):
        dst = m.at[mine, six, tile_of(before(k), t)]
        src = xin.at[:, pl.ds(p_here, 6), 8 * t : 8 * t + 8, cols(ty)] if first else dst
        return rcopy(src, dst, csend.at[2 * k + t], crecv.at[2 * k + t], cdev)

    def cfcopy(k, t):
        ref = m.at[far, six, tile_of(before(k), t)]
        return rcopy(ref, ref, csend.at[8 + 2 * k + t], crecv.at[8 + 2 * k + t], cdev)

    def hcopy(k):
        return rcopy(
            yhs.at[after(k)], yh.at[sp, rows(ty)], hsend.at[k], hrecv.at[k], (sp, tx, after(k))
        )

    def xcopy(side, y):
        return rcopy(
            xhs.at[y], xb.at[sp, side], xsend.at[4 * side + y], xrecv.at[side],
            (sp, tx + 1 if side == 0 else tx - 1, y),
        )

    zcopy(0, 0, True).start()
    zcopy(0, 1, True).start()
    for k, t in Y_ORDER[:2]:
        ycopy(k, t).start()
    for side, cond in ((0, up), (1, down)):

        @pl.when(cond)
        def _(side=side):
            for y in range(4):
                xcopy(side, y).start()

    for k in (2, 1, 3):
        hcopy(k).start()
    for k, t in Y_ORDER[2:4]:
        ycopy(k, t).start()
    ecopy(1).start()
    ecopy(3).start()
    for k, t in Y_ORDER[4:]:
        ycopy(k, t).start()
    ecopy(2).start()
    for t in range(2):
        ccopy(0, t, True).start()
    own = pltpu.make_async_copy(
        xin.at[:, pl.ds(p_here, 6), :, cols(ty)], m.at[mine, six, rows(ty)], lsem.at[0]
    )
    own.start()
    ownh = pltpu.make_async_copy(yhs.at[ty], yh.at[sp, rows(ty)], lsem.at[1])
    ownh.start()
    own.wait()
    ownh.wait()

    def xrows(first):
        return pl.ds(pl.multiple_of(first * 4, 8), 32)

    def xz():
        ref = xb.at[sp, :, xrows(p_there)]
        return rcopy(ref, ref, hsend.at[4], hrecv.at[4], zdev)

    def yz():
        ref = yh.at[sp, 0:64]
        return rcopy(ref, ref, hsend.at[5], hrecv.at[5], zdev)

    def xc(q, who):
        ref = xb.at[who, :, xrows(p_here)]
        return rcopy(ref, ref, hsend.at[6 + q], hrecv.at[6 + q], cdev)

    def yc(q, who):
        ref = yh.at[who, 0:64]
        return rcopy(ref, ref, hsend.at[8 + q], hrecv.at[8 + q], cdev)

    for k, t in Y_ORDER[:2]:
        ycopy(k, t).wait_recv()
        zcopy(k, t).start()
    for k in (1, 3, 2):
        hcopy(k).wait_recv()
    yz().start()
    yc(0, sp).start()
    for side, cond in ((0, tx > 0), (1, tx < 7)):

        @pl.when(cond)
        def _(side=side):
            xcopy(side, 0).wait_recv()

    xz().start()
    xc(0, sp).start()
    for k, t in Y_ORDER[2:4]:
        ycopy(k, t).wait_recv()
        zcopy(k, t).start()
    for t in range(2):
        zcopy(0, t).wait_recv()
        cfcopy(0, t).start()
    yz().wait_recv()
    yc(1, zsp).start()
    for k in (1, 3):
        ecopy(k).wait_recv()
        for t in range(2):
            ccopy(k, t).start()
    for q in range(2):
        yc(q, sp).wait_recv()
    for t in range(2):
        ccopy(0, t).wait_recv()
        cfcopy(0, t).wait_recv()

    row8 = lax.broadcasted_iota(jnp.int32, (8, 128), 0)
    lane8 = lax.broadcasted_iota(jnp.int32, (8, 128), 1)

    def stage1(rt, wrap=False):
        tile = pl.ds(pl.multiple_of(rt * 8, 8), 8)
        dsts = [pl.ds(pl.multiple_of(rt * 8 + 8, 8), 8)] + [pl.ds(0, 8)] * wrap
        for ct in range(2):
            v = [[m[i, 2 * sp + k, tile, ct * 128 : ct * 128 + 128] for k in range(6)] for i in range(S)]
            for f, (i, j) in enumerate(FIELDS):
                p = v[i] if j is None else [a * b for a, b in zip(v[i], v[j])]
                mid = (p[1] + p[2]) + (p[3] + p[4])
                for dst in dsts:
                    zs[2 * f, ct, dst, :] = p[0] + mid
                    zs[2 * f + 1, ct, dst, :] = mid + p[5]
        h = [
            pltpu.roll(yh[i // 2, tile, :], lax.rem(256 - 48 * (i % 2) - 8 * sp, 128), 1) for i in range(S)
        ]
        for f, (i, j) in enumerate(FIELDS):
            for dst in dsts:
                zh[f, dst, :] = h[i] if j is None else h[i] * h[j]

    def halos():
        xz().wait_recv()
        xc(1, zsp).start()
        for q in range(2):
            xc(q, sp).wait_recv()
        for i in range(S):
            for z in range(NZ):
                r = 4 * z + 2 * (i % 2) + (8 if z >= 4 else 0)
                m[i, 2 + z, 64:66, :] = xb[i // 2, 1, r : r + 2, :]
                m[i, 2 + z, 70:72, :] = xb[i // 2, 0, r : r + 2, :]
        for q in range(4):
            yh[q, 64:72] = jnp.where(row8 < 4, xb[q, 1, 16:24, 0:128], xb[q, 0, 16:24, 0:128])
        stage1(8, True)

    def span(pos, extent):
        return (jnp.minimum(pos + 2, extent - 1) - jnp.maximum(pos - 2, 0) + 1).astype(jnp.float32)

    def xsum(ref, x0):
        w = [ref[pl.ds(x0 * 8 + 6 + k, 8), :] for k in range(5)]
        return ((w[0] + w[1]) + (w[2] + w[3])) + w[4]

    def banded(v, w):
        hi = v.astype(jnp.bfloat16)
        rest = v - hi.astype(jnp.float32)
        mid = rest.astype(jnp.bfloat16)
        low = (rest - mid.astype(jnp.float32)).astype(jnp.bfloat16)
        hi, mid, low = (jnp.dot(q, w, preferred_element_type=jnp.float32) for q in (hi, mid, low))
        return hi + (mid + low)

    def stage2(x0):
        out_rows = pl.ds(pl.multiple_of(x0 * 8, 8), 8)
        for g in range(2 * NF):
            for ct in range(2):
                xs[g * 8 : g * 8 + 8, ct * 128 : ct * 128 + 128] = xsum(zs.at[g, ct], x0)
        for f in range(NF):
            hs[f * 8 : f * 8 + 8, :] = xsum(zh.at[f], x0)
        ys[...] = banded(xs[...], band[...])
        hy[...] = banded(hs[...], hband[...])
        cx_ = span(tx * ROWS + x0 * 8 + row8, NX)
        for p in range(2):
            cz = span(2 * sp + p, NZ)
            inv = [1.0 / (cx_ * span(ty * COLS + ct * 128 + lane8, NY) * cz) for ct in range(2)]

            def box(f):
                g = 8 * (2 * f + p)
                c = hy[8 * f : 8 * f + 8, 128 * p : 128 * p + 128]
                return (
                    (ys[g : g + 8, 0:128] + jnp.where(lane8 < 2, c, 0.0)) * inv[0],
                    (ys[g : g + 8, 128:256] + jnp.where(lane8 >= 126, c, 0.0)) * inv[1],
                )

            means = [box(i) for i in range(S)]
            var = []
            for i in range(S):
                sq = box(S + i)
                var.append(tuple(sq[t] - means[i][t] * means[i][t] + EPS for t in range(2)))
            for n, (i, j) in enumerate(PAIRS):
                pr = box(2 * S + n)
                for t in range(2):
                    cov = pr[t] - means[i][t] * means[j][t]
                    o_ref[n, p, out_rows, t * 128 : t * 128 + 128] = cov * lax.rsqrt(var[i][t] * var[j][t])

    def pick(u, values):
        return sum(v * (u == n).astype(jnp.int32) for n, v in enumerate(values) if v)

    def unit_of(r):
        k = lax.rem(ty + 4 - lax.div(r, 2), 4)
        q = 2 * k + lax.rem(r, 2)
        return pick(q, [UNITS.index((n // 2, n % 2)) for n in range(8)])

    def step(u, _):
        k, t = pick(u, [k for k, _ in UNITS]), pick(u, [t for _, t in UNITS])

        @pl.when(jnp.logical_and(u >= 2, u < 8))
        def _():
            zcopy(k, t).wait_recv()
            cfcopy(k, t).start()

        for n, (ky, t_y) in ((3, Y_ORDER[4]), (4, Y_ORDER[5])):

            @pl.when(u == n)
            def _(ky=ky, t_y=t_y):
                ycopy(ky, t_y).wait_recv()
                zcopy(ky, t_y).start()

        @pl.when(u == 5)
        def _():
            ecopy(2).wait_recv()
            for t in range(2):
                ccopy(2, t).start()

        @pl.when(u >= 1)
        def _():
            now = u - 1
            k, t = pick(now, [k for k, _ in UNITS]), pick(now, [t for _, t in UNITS])
            rt = 2 * before(k) + t

            @pl.when(now >= 2)
            def _():
                ccopy(k, t).wait_recv()
                cfcopy(k, t).wait_recv()

            stage1(rt)

            @pl.when(now == 1)
            def _():
                halos()

            def near(d, _):
                x0 = rt - 1 + d
                inside = jnp.logical_and(x0 >= 0, x0 < 8)
                done = jnp.maximum(unit_of(x0), jnp.maximum(unit_of(jnp.maximum(x0 - 1, 0)), unit_of(jnp.minimum(x0 + 1, 7))))

                @pl.when(jnp.logical_and(inside, done == now))
                def _():
                    stage2(x0)

                return 0

            lax.fori_loop(0, 3, near, 0)

        return 0

    lax.fori_loop(0, 9, step, 0)
    for k in range(4):
        for t in range(2):
            zcopy(k, t).wait_send()
            ccopy(k, t).wait_send()
            cfcopy(k, t).wait_send()
            if k:
                ycopy(k, t).wait_send()
        if k:
            ecopy(k).wait_send()
            hcopy(k).wait_send()
    xz().wait_send()
    yz().wait_send()
    for q in range(2):
        for c in (xc(q, sp), yc(q, sp)):
            c.wait_send()
    for side, cond in ((0, up), (1, down)):

        @pl.when(cond)
        def _(side=side):
            for y in range(4):
                xcopy(side, y).wait_send()


def shards(x):
    f32 = jnp.float32
    return pl.pallas_call(
        kernel,
        out_shape=jax.ShapeDtypeStruct((len(PAIRS), 2, ROWS, COLS), f32),
        in_specs=[pl.BlockSpec(memory_space=pltpu.VMEM)],
        out_specs=pl.BlockSpec(memory_space=pltpu.VMEM),
        scratch_shapes=[
            pltpu.VMEM((S, 12, 72, COLS), f32),
            pltpu.VMEM((4, 72, 128), f32),
            pltpu.VMEM((4, 2, 40, COLS), f32),
            pltpu.VMEM((4, BLK, 128), f32),
            pltpu.VMEM((4, 40, COLS), f32),
            pltpu.VMEM((2 * NF, 2, 80, 128), f32),
            pltpu.VMEM((NF, 80, 128), f32),
            pltpu.VMEM((16 * NF, COLS), f32),
            pltpu.VMEM((16 * NF, COLS), f32),
            pltpu.VMEM((8 * NF, 128), f32),
            pltpu.VMEM((8 * NF, COLS), f32),
            pltpu.VMEM((COLS, COLS), jnp.bfloat16),
            pltpu.VMEM((128, COLS), jnp.bfloat16),
        ]
        + [pltpu.SemaphoreType.DMA((n,)) for n in (8, 8, 4, 4, 8, 8, 16, 16, 10, 10, 8, 2, 2)],
        name="correlate",
        compiler_params=pltpu.CompilerParams(
            collective_id=0, has_side_effects=True, vmem_limit_bytes=48 << 20
        ),
    )(x)


def solution(mesh):
    return jax.shard_map(
        shards,
        mesh=mesh,
        in_specs=(P("sp", None, ("tx", "ty"), None),),
        out_specs=P(None, "sp", "tx", "ty"),
        check_vma=False,
    )
```

```python
import jax
import jax.numpy as jnp
from jax import lax
from jax.experimental import pallas as pl
from jax.experimental.pallas import tpu as pltpu
from jax.sharding import PartitionSpec as P

EPS = 1e-06
MESH = pl.DeviceIdType.MESH
S, NZ, NX, NY = 8, 8, 512, 1024
ROWS, COLS, BLK = 64, 256, 16
PAIRS = [(i, j) for i in range(S) for j in range(i + 1, S)]
FIELDS = [(i, None) for i in range(S)] + [(i, i) for i in range(S)] + PAIRS
NF = len(FIELDS)
Y_ORDER = ((1, 1), (3, 0), (1, 0), (3, 1))
K_UNITS = (0, 0, 1, 3, 1, 3, 2, 2)
T_UNITS = (0, 1, 1, 0, 0, 1)
GROUPS = (((5, 0), (6, 5), (7, 3)), ((4, 0), (5, 2), (7, 5)), ((4, 3), (5, 5), (7, 0)), ((4, 5), (6, 0), (7, 2)))
GROUP = 3
HALO_UNIT = 3


def kernel(
    x, o_ref, xin, m, yh, xb, yhs, xhs, yz, lhs, rhs, tmp,
    ysend, yrecv, esend, erecv, zsend, zrecv, csend, crecv, hsend, hrecv, xsend, xrecv, lsem,
):
    sp, tx, ty = (lax.axis_index(a) for a in ("sp", "tx", "ty"))
    zhi = lax.div(sp, 2)
    core = lax.rem(sp, 2)
    zsp = lax.rem(sp + 2, 4)
    csp = sp + 1 - 2 * core
    p_here = 2 * zhi
    p_there = 2 - 2 * zhi
    p_extra = 6 * zhi

    def after(k):
        return lax.rem(ty + k, 4)

    def before(k):
        return lax.rem(ty + 4 - k, 4)

    up = jnp.logical_and(ty == 3, tx < 7)
    down = jnp.logical_and(ty == 0, tx > 0)

    barrier = pltpu.get_barrier_semaphore()

    def greet(*dev):
        pl.semaphore_signal(barrier, inc=1, device_id=dev, device_id_type=MESH)

    for k in (2, 1, 3):
        greet(sp, tx, after(k))
    greet(zsp, tx, ty)
    greet(csp, tx, ty)

    @pl.when(tx > 0)
    def _():
        greet(sp, tx - 1, 3)

    @pl.when(tx < 7)
    def _():
        greet(sp, tx + 1, 0)

    load = pltpu.make_async_copy(x, xin, lsem.at[0])
    load.start()
    pl.semaphore_wait(barrier, 5 + 4 * up.astype(jnp.int32) + 4 * down.astype(jnp.int32))

    def rcopy(src, dst, ss, rs, dev):
        return pltpu.make_async_remote_copy(
            src_ref=src, dst_ref=dst, send_sem=ss, recv_sem=rs, device_id=dev, device_id_type=MESH
        )

    def cols(y):
        return pl.ds(pl.multiple_of(y * COLS, COLS), COLS)

    def tile_of(b, t):
        return pl.ds(pl.multiple_of(b * BLK + 8 * t, 8), 8)

    def pick(u, values):
        return sum(v * (u == n).astype(jnp.int32) for n, v in enumerate(values))

    t_sent, t_got = pick(ty, (0, 0, 1)), pick(ty, (1,))

    def eight(b):
        return pl.ds(pl.multiple_of(b * 8, 8), 8)

    zdev = (zsp, tx, ty)
    cdev = (csp, tx, ty)
    mine = pl.ds(2 * sp, 2)
    far = pl.ds(2 * zsp, 2)
    six = pl.ds(p_here + 2, 6)
    six_there = pl.ds(p_there + 2, 6)
    own_rows = pl.ds(pl.multiple_of(ty * BLK, BLK), BLK)

    def ycopy(k, t):
        return rcopy(
            x.at[:, pl.ds(p_there, 6), eight(t), cols(after(k))],
            m.at[mine, six_there, tile_of(ty, t)],
            ysend.at[2 * k + t], yrecv.at[2 * k + t], (sp, tx, after(k)),
        )

    def ecopy(k):
        return rcopy(
            x.at[:, pl.ds(p_extra, 2), :, cols(after(k))],
            m.at[mine, pl.ds(p_extra + 2, 2), own_rows],
            esend.at[k], erecv.at[k], (sp, tx, after(k)),
        )

    def zcopy(k, t, first=False):
        dst = m.at[mine, six_there, tile_of(before(k), t)]
        src = x.at[:, pl.ds(p_there, 6), 8 * t : 8 * t + 8, cols(ty)] if first else dst
        return rcopy(src, dst, zsend.at[2 * k + t], zrecv.at[2 * k + t], zdev)

    def ccopy(k, t, first=False):
        dst = m.at[mine, six, tile_of(before(k), t)]
        src = x.at[:, pl.ds(p_here, 6), 8 * t : 8 * t + 8, cols(ty)] if first else dst
        return rcopy(src, dst, csend.at[2 * k + t], crecv.at[2 * k + t], cdev)

    def cfcopy(k, t):
        ref = m.at[far, six, tile_of(before(k), t)]
        return rcopy(ref, ref, csend.at[8 + 2 * k + t], crecv.at[8 + 2 * k + t], cdev)

    def hcopy(k):
        return rcopy(yhs.at[after(k)], yh.at[sp, eight(ty)], hsend.at[k], hrecv.at[k], (sp, tx, after(k)))

    def xcopies(side, y):
        dev = (sp, tx + 1 if side == 0 else tx - 1, y)
        q = 2 * (4 * side + y)
        return (
            rcopy(xhs.at[y], xb.at[sp, side], xsend.at[q], xrecv.at[2 * side], dev),
            rcopy(
                yhs.at[y], yh.at[sp, 32 + 8 * side : 40 + 8 * side],
                xsend.at[q + 1], xrecv.at[2 * side + 1], dev,
            ),
        )

    def xrows(first):
        return pl.ds(pl.multiple_of(first * 4, 8), 24)

    def xz():
        ref = xb.at[sp, :, xrows(p_there)]
        return rcopy(ref, ref, hsend.at[4], hrecv.at[4], zdev)

    def yzcopy():
        return rcopy(yh.at[sp], yh.at[sp], hsend.at[5], hrecv.at[5], zdev)

    def xc(q, who):
        ref = xb.at[who, :, xrows(p_here)]
        return rcopy(ref, ref, hsend.at[6 + q], hrecv.at[6 + q], cdev)

    def yc(q, who):
        return rcopy(yh.at[who], yh.at[who], hsend.at[8 + q], hrecv.at[8 + q], cdev)

    zcopy(0, 0, True).start()
    zcopy(0, 1, True).start()
    for k, t in Y_ORDER[:2]:
        ycopy(k, t).start()

    load.wait()
    row8 = lax.broadcasted_iota(jnp.int32, (8, 128), 0)
    lane8 = lax.broadcasted_iota(jnp.int32, (8, 128), 1)
    zero = jnp.zeros((8, 128), jnp.float32)
    for y in range(4):
        acc = zero
        for t in range(2):
            for s in range(2):
                for z in range(NZ):
                    base = 64 * t + 32 * s + 4 * z
                    at = slice(8 * t, 8 * t + 8)
                    left = xin[s, z, at, y * COLS - 128 : y * COLS] if y > 0 else zero
                    right = xin[s, z, at, y * COLS + COLS : y * COLS + COLS + 128] if y < 3 else zero
                    if y < 3:
                        right = pltpu.roll(right, base, 1) if base else right
                    if y > 0:
                        left = pltpu.roll(left, (base + 4) % 128, 1) if base != 124 else left
                    acc = jnp.where(jnp.logical_and(lane8 >= base, lane8 < base + 2), right, acc)
                    acc = jnp.where(jnp.logical_and(lane8 >= base + 2, lane8 < base + 4), left, acc)
        yhs[y] = acc

    def pack_rows(first):
        for y in range(4):
            for z in range(NZ):
                for s in range(2):
                    r = 4 * z + 2 * s
                    xhs[y, r : r + 2, :] = xin[s, z, first : first + 2, y * COLS : (y + 1) * COLS]

    for side, cond, first in ((0, up, 14), (1, down, 0)):

        @pl.when(cond)
        def _(side=side, first=first):
            pack_rows(first)
            for y in range(4):
                for c in xcopies(side, y):
                    c.start()

    for k in (2, 1, 3):
        hcopy(k).start()
    for k, t in Y_ORDER[2:]:
        ycopy(k, t).start()
    ecopy(1).start()
    ecopy(3).start()
    ycopy(2, t_sent).start()
    ycopy(2, 1 - t_sent).start()
    ecopy(2).start()
    for t in range(2):
        ccopy(0, t, True).start()
    own = pltpu.make_async_copy(
        x.at[:, pl.ds(p_here, 6), :, cols(ty)], m.at[mine, six, own_rows], lsem.at[1]
    )
    own.start()
    yh[sp, eight(ty)] = yhs[ty]

    for s in range(S):
        m[s, 0:2] = jnp.zeros((2, 72, COLS), jnp.float32)
        m[s, 10:12] = jnp.zeros((2, 72, COLS), jnp.float32)

    for side, cond in ((0, tx == 0), (1, tx == 7)):

        @pl.when(cond)
        def _(side=side):
            xb[sp, side] = jnp.zeros((32, COLS), jnp.float32)
            yh[sp, 32 + 8 * side : 40 + 8 * side] = zero

    for k, t in Y_ORDER[:2]:
        ycopy(k, t).wait_recv()
        zcopy(k, t).start()
    for k in (1, 3, 2):
        hcopy(k).wait_recv()
    for side, cond in ((0, tx > 0), (1, tx < 7)):

        @pl.when(cond)
        def _(side=side):
            for c in xcopies(side, 0):
                c.wait_recv()

    yzcopy().start()
    yc(0, sp).start()
    xz().start()
    xc(0, sp).start()
    for k, t in Y_ORDER[2:4]:
        ycopy(k, t).wait_recv()
        zcopy(k, t).start()

    r_at = lax.broadcasted_iota(jnp.int32, (COLS, COLS), 0)
    c_at = lax.broadcasted_iota(jnp.int32, (COLS, COLS), 1)
    band = jnp.where(jnp.abs(r_at - c_at) <= 2, 1.0, 0.0).astype(jnp.bfloat16)
    r_at = lax.broadcasted_iota(jnp.int32, (128, COLS), 0)
    c_at = lax.broadcasted_iota(jnp.int32, (128, COLS), 1)
    plane, kind = lax.div(r_at, 4), lax.rem(r_at, 4)
    ends = (
        ((kind == 0) & (c_at >= COLS - 2))
        | ((kind == 1) & (c_at == COLS - 1))
        | ((kind == 2) & (c_at == 0))
        | ((kind == 3) & (c_at <= 1))
    )
    for p in range(2):
        part = jnp.where(ends & (plane >= p) & (plane <= p + 4), 1.0, 0.0).astype(jnp.bfloat16)
        for q in range(3):
            rhs[p, 256 * q : 256 * q + 256, :] = band
            rhs[p, 768 + 128 * q : 896 + 128 * q, :] = part

    for t in range(2):
        zcopy(0, t).wait_recv()
        cfcopy(0, t).start()
    yzcopy().wait_recv()
    yc(1, zsp).start()
    for k in (1, 3):
        ecopy(k).wait_recv()
        for t in range(2):
            ccopy(k, t).start()
    own.wait()
    for q in range(2):
        yc(q, sp).wait_recv()
    for t in range(2):
        ccopy(0, t).wait_recv()
        cfcopy(0, t).wait_recv()

    def split(v):
        hi = v.astype(jnp.bfloat16)
        rest = v - hi.astype(jnp.float32)
        mid = rest.astype(jnp.bfloat16)
        return hi, mid, (rest - mid.astype(jnp.float32)).astype(jnp.bfloat16)

    def halo_cols(i, rows, t):
        h = pltpu.roll(yh[i // 2, rows, :], lax.rem(264 - 64 * t - 32 * (i % 2) - 8 * sp, 128), 1)
        at = 2 * sp - 2 + lax.div(lane8, 4)
        return jnp.where((at >= 0) & (at < NZ), h, 0.0)

    def stage1(rt, h, wrap=False):
        tile = pl.ds(pl.multiple_of(rt * 8, 8), 8)
        dsts = [pl.ds(pl.multiple_of(rt * 8 + 8, 8), 8)] + [pl.ds(0, 8)] * wrap
        for ct in range(2):
            v = [[m[i, 2 * sp + k, tile, ct * 128 : ct * 128 + 128] for k in range(6)] for i in range(S)]
            for f in range(0, NF, 2):
                sums = [[], []]
                for i, j in FIELDS[f : f + 2]:
                    p = v[i] if j is None else [a * b for a, b in zip(v[i], v[j])]
                    mid = (p[1] + p[2]) + (p[3] + p[4])
                    sums[0].append(p[0] + mid)
                    sums[1].append(mid + p[5])
                for p in range(2):
                    for q, part in enumerate(split(jnp.concatenate(sums[p], 0))):
                        at = 256 * q + 128 * ct
                        lhs[p, 8 * f : 8 * f + 16, at : at + 128] = part
        for f in range(0, NF, 2):
            hv = [h[i] if j is None else h[i] * h[j] for i, j in FIELDS[f : f + 2]]
            for q, part in enumerate(split(jnp.concatenate(hv, 0))):
                for p in range(2):
                    lhs[p, 8 * f : 8 * f + 16, 768 + 128 * q : 896 + 128 * q] = part
        for p in range(2):
            r = jnp.dot(lhs[p], rhs[p], preferred_element_type=jnp.float32)
            for f in range(NF):
                for ct in range(2):
                    for dst in dsts:
                        yz[2 * f + p, ct, dst, :] = r[8 * f : 8 * f + 8, 128 * ct : 128 * ct + 128]

    def halos():
        xz().wait_recv()
        xc(1, zsp).start()
        for q in range(2):
            xc(q, sp).wait_recv()
        for i in range(S):
            for z in range(NZ):
                r = 4 * z + 2 * (i % 2)
                m[i, 2 + z, 64:66, :] = xb[i // 2, 1, r : r + 2, :]
                m[i, 2 + z, 70:72, :] = xb[i // 2, 0, r : r + 2, :]
        h = [
            jnp.where(row8 < 4, halo_cols(i, slice(40, 48), 0), halo_cols(i, slice(32, 40), 1)) for i in range(S)
        ]
        stage1(8, h, True)

    def span(pos, extent):
        return (jnp.minimum(pos + 2, extent - 1) - jnp.maximum(pos - 2, 0) + 1).astype(jnp.float32)

    def stage2(x0):
        start = x0 * 8
        for p in range(2):
            cz = span(2 * sp + p, NZ)
            for ct in range(2):
                cy = span(ty * COLS + ct * 128 + lane8, NY) * cz
                inv = [1.0 / (span(tx * ROWS + start + row8 * GROUP + q, NX) * cy) for q in range(GROUP)]

                def box(f):
                    w = [yz[2 * f + p, ct, pl.ds(start + 6 + q, 8, stride=GROUP), :] for q in range(GROUP + 4)]
                    a = [w[q] + w[q + 1] for q in range(GROUP + 3)]
                    return [((a[q] + a[q + 2]) + w[q + 4]) * inv[q] for q in range(GROUP)]

                means = [box(i) for i in range(S)]
                var = [[b - u * u + EPS for b, u in zip(box(S + i), means[i])] for i in range(S)]
                for n, (i, j) in enumerate(PAIRS):
                    b = box(2 * S + n)
                    for q in range(GROUP):
                        cov = b[q] - means[i][q] * means[j][q]
                        tmp[n, pl.ds(q, 8, stride=GROUP), :] = cov * lax.rsqrt(var[i][q] * var[j][q])
                for n in range(len(PAIRS)):
                    o_ref[n, p, pl.ds(pl.multiple_of(start, 8), 8 * GROUP), ct * 128 : ct * 128 + 128] = tmp[n]

    def unit(u):
        return pick(u, K_UNITS), pick(u, T_UNITS + (t_got, 1 - t_got))

    def step(u, _):
        @pl.when(jnp.logical_and(u >= 2, u < 8))
        def _():
            k, t = unit(u)
            zcopy(k, t).wait_recv()
            cfcopy(k, t).start()

        for n, t in ((3, t_got), (4, 1 - t_got)):

            @pl.when(u == n)
            def _(t=t):
                ycopy(2, t).wait_recv()
                zcopy(2, t).start()

        @pl.when(u == 5)
        def _():
            ecopy(2).wait_recv()
            for t in range(2):
                ccopy(2, t).start()

        @pl.when(u >= 1)
        def _():
            k, t = unit(u - 1)
            b = before(k)

            @pl.when(u >= 3)
            def _():
                ccopy(k, t).wait_recv()
                cfcopy(k, t).wait_recv()

            stage1(2 * b + t, [halo_cols(i, eight(b), t) for i in range(S)])

            @pl.when(u - 1 == HALO_UNIT)
            def _():
                halos()

            group = sum(
                (g0 + 1) * ((ty == y) & (u - 1 == n)).astype(jnp.int32) for y in range(4) for n, g0 in GROUPS[y]
            )

            @pl.when(group > 0)
            def _():
                stage2(group - 1)

        return 0

    lax.fori_loop(0, 9, step, 0)

    for k in range(4):
        for t in range(2):
            zcopy(k, t).wait_send()
            ccopy(k, t).wait_send()
            cfcopy(k, t).wait_send()
            if k:
                ycopy(k, t).wait_send()
        if k:
            ecopy(k).wait_send()
            hcopy(k).wait_send()
    xz().wait_send()
    yzcopy().wait_send()
    for q in range(2):
        for c in (xc(q, sp), yc(q, sp)):
            c.wait_send()
    for side, cond in ((0, up), (1, down)):

        @pl.when(cond)
        def _(side=side):
            for y in range(4):
                for c in xcopies(side, y):
                    c.wait_send()


def shards(x):
    f32 = jnp.float32
    return pl.pallas_call(
        kernel,
        out_shape=jax.ShapeDtypeStruct((len(PAIRS), 2, ROWS, COLS), f32),
        in_specs=[pl.BlockSpec(memory_space=pltpu.HBM)],
        out_specs=pl.BlockSpec(memory_space=pltpu.VMEM),
        scratch_shapes=[
            pltpu.VMEM((2, NZ, BLK, NY), f32),
            pltpu.VMEM((S, 12, 72, COLS), f32),
            pltpu.VMEM((4, 48, 128), f32),
            pltpu.VMEM((4, 2, 32, COLS), f32),
            pltpu.VMEM((4, 8, 128), f32),
            pltpu.VMEM((4, 32, COLS), f32),
            pltpu.VMEM((2 * NF, 2, 80, 128), f32),
            pltpu.VMEM((2, 8 * NF, 1152), jnp.bfloat16),
            pltpu.VMEM((2, 1152, COLS), jnp.bfloat16),
            pltpu.VMEM((len(PAIRS), 8 * GROUP, 128), f32),
        ]
        + [pltpu.SemaphoreType.DMA((n,)) for n in (8, 8, 4, 4, 8, 8, 16, 16, 10, 10, 16, 4, 2)],
        name="correlate",
        compiler_params=pltpu.CompilerParams(
            collective_id=0, has_side_effects=True, vmem_limit_bytes=48 << 20
        ),
    )(pltpu.with_memory_space_constraint(x, pltpu.HBM))


def solution(mesh):
    return jax.shard_map(
        shards,
        mesh=mesh,
        in_specs=(P("sp", None, ("tx", "ty"), None),),
        out_specs=P(None, "sp", "tx", "ty"),
        check_vma=False,
    )
```

```python
import jax
import jax.numpy as jnp
from jax import lax
from jax.experimental import pallas as pl
from jax.experimental.pallas import tpu as pltpu
from jax.sharding import PartitionSpec as P

EPS = 1e-06
MESH = pl.DeviceIdType.MESH
S, NZ, NX, NY = 8, 8, 512, 1024
ROWS, COLS, BLK = 64, 256, 16
PAIRS = [(i, j) for i in range(S) for j in range(i + 1, S)]
FIELDS = [(i, None) for i in range(S)] + [(i, i) for i in range(S)] + PAIRS
NF = len(FIELDS)
Y_ORDER = ((1, 1), (3, 0), (1, 0), (3, 1))
GROUPS = (((5, 0), (6, 5), (7, 3)), ((4, 0), (5, 2), (7, 5)), ((4, 3), (5, 5), (7, 0)), ((4, 5), (6, 0), (7, 2)))
GROUP = 3
COLUMNS, CORNERS = slice(0, 32), slice(32, 48)
HALO_UNIT = 4


def kernel(
    x, o_ref, xin, m, yh, xb, yhs, xhs, yz, lhs, rhs, tmp,
    ysend, yrecv, esend, erecv, zsend, zrecv, csend, crecv, hsend, hrecv, xsend, xrecv, lsem,
):
    sp, tx, ty = (lax.axis_index(a) for a in ("sp", "tx", "ty"))
    zhi = lax.div(sp, 2)
    core = lax.rem(sp, 2)
    zsp = lax.rem(sp + 2, 4)
    csp = sp + 1 - 2 * core
    p_here = 2 * zhi
    p_there = 2 - 2 * zhi
    p_extra = 6 * zhi

    def after(k):
        return lax.rem(ty + k, 4)

    def before(k):
        return lax.rem(ty + 4 - k, 4)

    up = jnp.logical_and(ty == 3, tx < 7)
    down = jnp.logical_and(ty == 0, tx > 0)

    barrier = pltpu.get_barrier_semaphore()

    def greet(*dev):
        pl.semaphore_signal(barrier, inc=1, device_id=dev, device_id_type=MESH)

    for k in (2, 1, 3):
        greet(sp, tx, after(k))
        greet(zsp, tx, after(k))
    greet(zsp, tx, ty)
    greet(csp, tx, ty)

    @pl.when(tx > 0)
    def _():
        greet(sp, tx - 1, 3)

    @pl.when(tx < 7)
    def _():
        greet(sp, tx + 1, 0)

    load = pltpu.make_async_copy(x, xin, lsem.at[0])
    load.start()
    pl.semaphore_wait(barrier, 8 + 4 * up.astype(jnp.int32) + 4 * down.astype(jnp.int32))

    def rcopy(src, dst, ss, rs, dev):
        return pltpu.make_async_remote_copy(
            src_ref=src, dst_ref=dst, send_sem=ss, recv_sem=rs, device_id=dev, device_id_type=MESH
        )

    def cols(y):
        return pl.ds(pl.multiple_of(y * COLS, COLS), COLS)

    def tile_of(b, t):
        return pl.ds(pl.multiple_of(b * BLK + 8 * t, 8), 8)

    def pick(u, values):
        return sum(v * (u == n).astype(jnp.int32) for n, v in enumerate(values))

    t_sent, t_got = pick(ty, (0, 0, 1)), pick(ty, (1,))
    turn = pick(ty, (1,))
    k_units = (0, 0) + (1 + 2 * turn, 3 - 2 * turn) * 2 + (2, 2)
    t_units = (0, 1, 1 - turn, turn, turn, 1 - turn, t_got, 1 - t_got)

    def eight(b):
        return pl.ds(pl.multiple_of(b * 8, 8), 8)

    zdev = (zsp, tx, ty)
    cdev = (csp, tx, ty)
    mine = pl.ds(2 * sp, 2)
    far = pl.ds(2 * zsp, 2)
    six = pl.ds(p_here + 2, 6)
    six_there = pl.ds(p_there + 2, 6)
    own_rows = pl.ds(pl.multiple_of(ty * BLK, BLK), BLK)

    def ycopy(k, t):
        return rcopy(
            x.at[:, pl.ds(p_there, 6), eight(t), cols(after(k))],
            m.at[mine, six_there, tile_of(ty, t)],
            ysend.at[2 * k + t], yrecv.at[2 * k + t], (sp, tx, after(k)),
        )

    def ecopy(k):
        return rcopy(
            x.at[:, pl.ds(p_extra, 2), :, cols(after(k))],
            m.at[mine, pl.ds(p_extra + 2, 2), own_rows],
            esend.at[k], erecv.at[k], (sp, tx, after(k)),
        )

    def zcopy(k, t, first=False):
        dst = m.at[mine, six_there, tile_of(before(k), t)]
        src = x.at[:, pl.ds(p_there, 6), 8 * t : 8 * t + 8, cols(ty)] if first else dst
        return rcopy(src, dst, zsend.at[2 * k + t], zrecv.at[2 * k + t], zdev)

    def ccopy(k, t, first=False):
        dst = m.at[mine, six, tile_of(before(k), t)]
        src = x.at[:, pl.ds(p_here, 6), 8 * t : 8 * t + 8, cols(ty)] if first else dst
        return rcopy(src, dst, csend.at[2 * k + t], crecv.at[2 * k + t], cdev)

    def cfcopy(k, t):
        ref = m.at[far, six, tile_of(before(k), t)]
        return rcopy(ref, ref, csend.at[8 + 2 * k + t], crecv.at[8 + 2 * k + t], cdev)

    def hcopy(k, there):
        dev = (zsp if there else sp, tx, after(k))
        q = 4 * there + k
        return rcopy(yhs.at[after(k)], yh.at[sp, eight(ty)], hsend.at[q], hrecv.at[q], dev)

    def xcopies(side, y):
        dev = (sp, tx + 1 if side == 0 else tx - 1, y)
        q = 2 * (4 * side + y)
        return (
            rcopy(xhs.at[y], xb.at[sp, side], xsend.at[q], xrecv.at[2 * side], dev),
            rcopy(
                yhs.at[y], yh.at[sp, 32 + 8 * side : 40 + 8 * side],
                xsend.at[q + 1], xrecv.at[2 * side + 1], dev,
            ),
        )

    def xrows(first):
        return pl.ds(pl.multiple_of(first * 4, 8), 24)

    def xz():
        ref = xb.at[sp, :, xrows(p_there)]
        return rcopy(ref, ref, hsend.at[8], hrecv.at[8], zdev)

    def yzcopy():
        ref = yh.at[sp, CORNERS]
        return rcopy(ref, ref, hsend.at[9], hrecv.at[9], zdev)

    def xc(q, who):
        ref = xb.at[who, :, xrows(p_here)]
        return rcopy(ref, ref, hsend.at[10 + q], hrecv.at[10 + q], cdev)

    def yc(q, who, part):
        ref = yh.at[who, part]
        q = q + (12 if part is COLUMNS else 14)
        return rcopy(ref, ref, hsend.at[q], hrecv.at[q], cdev)

    zcopy(0, 0, True).start()
    for k, t in Y_ORDER[:2]:
        ycopy(k, t).start()

    load.wait()
    row8 = lax.broadcasted_iota(jnp.int32, (8, 128), 0)
    lane8 = lax.broadcasted_iota(jnp.int32, (8, 128), 1)
    zero = jnp.zeros((8, 128), jnp.float32)
    for y in range(4):
        acc = zero
        for t in range(2):
            for s in range(2):
                for z in range(NZ):
                    base = 64 * t + 32 * s + 4 * z
                    at = slice(8 * t, 8 * t + 8)
                    left = xin[s, z, at, y * COLS - 128 : y * COLS] if y > 0 else zero
                    right = xin[s, z, at, y * COLS + COLS : y * COLS + COLS + 128] if y < 3 else zero
                    if y < 3:
                        right = pltpu.roll(right, base, 1) if base else right
                    if y > 0:
                        left = pltpu.roll(left, (base + 4) % 128, 1) if base != 124 else left
                    acc = jnp.where(jnp.logical_and(lane8 >= base, lane8 < base + 2), right, acc)
                    acc = jnp.where(jnp.logical_and(lane8 >= base + 2, lane8 < base + 4), left, acc)
        yhs[y] = acc

    yh[sp, eight(ty)] = yhs[ty]
    for k in (2, 1, 3):
        hcopy(k, 1).start()
        hcopy(k, 0).start()
    hcopy(0, 1).start()

    def pack_rows(first):
        for y in range(4):
            for z in range(NZ):
                for s in range(2):
                    r = 4 * z + 2 * s
                    xhs[y, r : r + 2, :] = xin[s, z, first : first + 2, y * COLS : (y + 1) * COLS]

    for side, cond, first in ((0, up, 14), (1, down, 0)):

        @pl.when(cond)
        def _(side=side, first=first):
            pack_rows(first)
            for y in range(4):
                for c in xcopies(side, y):
                    c.start()

    zcopy(0, 1, True).start()
    for k, t in Y_ORDER[2:]:
        ycopy(k, t).start()
    ecopy(1).start()
    ecopy(3).start()
    ycopy(2, t_sent).start()
    ycopy(2, 1 - t_sent).start()
    ecopy(2).start()
    for t in range(2):
        ccopy(0, t, True).start()
    own = pltpu.make_async_copy(
        x.at[:, pl.ds(p_here, 6), :, cols(ty)], m.at[mine, six, own_rows], lsem.at[1]
    )
    own.start()

    for s in range(S):
        m[s, 0:2] = jnp.zeros((2, 72, COLS), jnp.float32)
        m[s, 10:12] = jnp.zeros((2, 72, COLS), jnp.float32)

    for side, cond in ((0, tx == 0), (1, tx == 7)):

        @pl.when(cond)
        def _(side=side):
            xb[sp, side] = jnp.zeros((32, COLS), jnp.float32)
            yh[sp, 32 + 8 * side : 40 + 8 * side] = zero

    for k, t in list(zip(k_units, t_units))[2:4]:
        ycopy(k, t).wait_recv()
        zcopy(k, t).start()
    for k in range(4):
        hcopy(k, 1).wait_recv()
        if k:
            hcopy(k, 0).wait_recv()
    yc(0, sp, COLUMNS).start()
    yc(1, zsp, COLUMNS).start()
    zcopy(0, 0).wait_recv()
    cfcopy(0, 0).start()
    for side, cond in ((0, tx > 0), (1, tx < 7)):

        @pl.when(cond)
        def _(side=side):
            for c in xcopies(side, 0):
                c.wait_recv()

    xz().start()
    yzcopy().start()
    xc(0, sp).start()
    yc(0, sp, CORNERS).start()
    for k, t in list(zip(k_units, t_units))[4:6]:
        ycopy(k, t).wait_recv()
        zcopy(k, t).start()

    r_at = lax.broadcasted_iota(jnp.int32, (COLS, COLS), 0)
    c_at = lax.broadcasted_iota(jnp.int32, (COLS, COLS), 1)
    band = jnp.where(jnp.abs(r_at - c_at) <= 2, 1.0, 0.0).astype(jnp.bfloat16)
    r_at = lax.broadcasted_iota(jnp.int32, (128, COLS), 0)
    c_at = lax.broadcasted_iota(jnp.int32, (128, COLS), 1)
    plane, kind = lax.div(r_at, 4), lax.rem(r_at, 4)
    ends = (
        ((kind == 0) & (c_at >= COLS - 2))
        | ((kind == 1) & (c_at == COLS - 1))
        | ((kind == 2) & (c_at == 0))
        | ((kind == 3) & (c_at <= 1))
    )
    for p in range(2):
        part = jnp.where(ends & (plane >= p) & (plane <= p + 4), 1.0, 0.0).astype(jnp.bfloat16)
        for q in range(3):
            rhs[p, 256 * q : 256 * q + 256, :] = band
            rhs[p, 768 + 128 * q : 896 + 128 * q, :] = part

    zcopy(0, 1).wait_recv()
    cfcopy(0, 1).start()
    own.wait()
    for q in range(2):
        yc(q, sp, COLUMNS).wait_recv()

    def split(v):
        hi = v.astype(jnp.bfloat16)
        rest = v - hi.astype(jnp.float32)
        mid = rest.astype(jnp.bfloat16)
        return hi, mid, (rest - mid.astype(jnp.float32)).astype(jnp.bfloat16)

    def halo_cols(i, rows, t):
        h = pltpu.roll(yh[i // 2, rows, :], lax.rem(264 - 64 * t - 32 * (i % 2) - 8 * sp, 128), 1)
        at = 2 * sp - 2 + lax.div(lane8, 4)
        return jnp.where((at >= 0) & (at < NZ), h, 0.0)

    def stage1(rt, h, wrap=False):
        tile = pl.ds(pl.multiple_of(rt * 8, 8), 8)
        dsts = [pl.ds(pl.multiple_of(rt * 8 + 8, 8), 8)] + [pl.ds(0, 8)] * wrap
        for ct in range(2):
            v = [[m[i, 2 * sp + k, tile, ct * 128 : ct * 128 + 128] for k in range(6)] for i in range(S)]
            for f in range(0, NF, 2):
                sums = [[], []]
                for i, j in FIELDS[f : f + 2]:
                    p = v[i] if j is None else [a * b for a, b in zip(v[i], v[j])]
                    mid = (p[1] + p[2]) + (p[3] + p[4])
                    sums[0].append(p[0] + mid)
                    sums[1].append(mid + p[5])
                for p in range(2):
                    for q, part in enumerate(split(jnp.concatenate(sums[p], 0))):
                        at = 256 * q + 128 * ct
                        lhs[p, 8 * f : 8 * f + 16, at : at + 128] = part
        for f in range(0, NF, 2):
            hv = [h[i] if j is None else h[i] * h[j] for i, j in FIELDS[f : f + 2]]
            for q, part in enumerate(split(jnp.concatenate(hv, 0))):
                for p in range(2):
                    lhs[p, 8 * f : 8 * f + 16, 768 + 128 * q : 896 + 128 * q] = part
        for p in range(2):
            r = jnp.dot(lhs[p], rhs[p], preferred_element_type=jnp.float32)
            for f in range(NF):
                for ct in range(2):
                    for dst in dsts:
                        yz[2 * f + p, ct, dst, :] = r[8 * f : 8 * f + 8, 128 * ct : 128 * ct + 128]

    def halos():
        for q in range(2):
            xc(q, sp).wait_recv()
            yc(q, sp, CORNERS).wait_recv()
        for i in range(S):
            for z in range(NZ):
                r = 4 * z + 2 * (i % 2)
                m[i, 2 + z, 64:66, :] = xb[i // 2, 1, r : r + 2, :]
                m[i, 2 + z, 70:72, :] = xb[i // 2, 0, r : r + 2, :]
        h = [
            jnp.where(row8 < 4, halo_cols(i, slice(40, 48), 0), halo_cols(i, slice(32, 40), 1)) for i in range(S)
        ]
        stage1(8, h, True)

    def span(pos, extent):
        return (jnp.minimum(pos + 2, extent - 1) - jnp.maximum(pos - 2, 0) + 1).astype(jnp.float32)

    def stage2(x0):
        start = x0 * 8
        for p in range(2):
            cz = span(2 * sp + p, NZ)
            for ct in range(2):
                cy = span(ty * COLS + ct * 128 + lane8, NY) * cz
                inv = [1.0 / (span(tx * ROWS + start + row8 * GROUP + q, NX) * cy) for q in range(GROUP)]

                def box(f):
                    w = [yz[2 * f + p, ct, pl.ds(start + 6 + q, 8, stride=GROUP), :] for q in range(GROUP + 4)]
                    a = [w[q] + w[q + 1] for q in range(GROUP + 3)]
                    return [((a[q] + a[q + 2]) + w[q + 4]) * inv[q] for q in range(GROUP)]

                means = [box(i) for i in range(S)]
                var = [[b - u * u + EPS for b, u in zip(box(S + i), means[i])] for i in range(S)]
                for n, (i, j) in enumerate(PAIRS):
                    b = box(2 * S + n)
                    for q in range(GROUP):
                        cov = b[q] - means[i][q] * means[j][q]
                        tmp[n, pl.ds(q, 8, stride=GROUP), :] = cov * lax.rsqrt(var[i][q] * var[j][q])
                for n in range(len(PAIRS)):
                    o_ref[n, p, pl.ds(pl.multiple_of(start, 8), 8 * GROUP), ct * 128 : ct * 128 + 128] = tmp[n]

    def unit(u):
        return pick(u, k_units), pick(u, t_units)

    def step(u, _):
        @pl.when(jnp.logical_and(u >= 2, u < 8))
        def _():
            k, t = unit(u)
            zcopy(k, t).wait_recv()
            cfcopy(k, t).start()

        for n, t in ((3, t_got), (4, 1 - t_got)):

            @pl.when(u == n)
            def _(t=t):
                ycopy(2, t).wait_recv()
                zcopy(2, t).start()

        for n, k in ((1, k_units[2]), (2, k_units[3]), (5, 2)):

            @pl.when(u == n)
            def _(k=k):
                ecopy(k).wait_recv()
                for t in range(2):
                    ccopy(k, t).start()

        @pl.when(u == HALO_UNIT)
        def _():
            xz().wait_recv()
            xc(1, zsp).start()
            yzcopy().wait_recv()
            yc(1, zsp, CORNERS).start()

        @pl.when(u >= 1)
        def _():
            k, t = unit(u - 1)
            b = before(k)

            ccopy(k, t).wait_recv()
            cfcopy(k, t).wait_recv()

            stage1(2 * b + t, [halo_cols(i, eight(b), t) for i in range(S)])

            @pl.when(u - 1 == HALO_UNIT)
            def _():
                halos()

            group = sum(
                (g0 + 1) * ((ty == y) & (u - 1 == n)).astype(jnp.int32) for y in range(4) for n, g0 in GROUPS[y]
            )

            @pl.when(group > 0)
            def _():
                stage2(group - 1)

        return 0

    lax.fori_loop(0, 9, step, 0)

    for k in range(4):
        for t in range(2):
            zcopy(k, t).wait_send()
            ccopy(k, t).wait_send()
            cfcopy(k, t).wait_send()
            if k:
                ycopy(k, t).wait_send()
        if k:
            ecopy(k).wait_send()
            hcopy(k, 0).wait_send()
        hcopy(k, 1).wait_send()
    xz().wait_send()
    yzcopy().wait_send()
    for q in range(2):
        for c in (xc(q, sp), yc(q, sp, COLUMNS), yc(q, sp, CORNERS)):
            c.wait_send()
    for side, cond in ((0, up), (1, down)):

        @pl.when(cond)
        def _(side=side):
            for y in range(4):
                for c in xcopies(side, y):
                    c.wait_send()


def shards(x):
    f32 = jnp.float32
    return pl.pallas_call(
        kernel,
        out_shape=jax.ShapeDtypeStruct((len(PAIRS), 2, ROWS, COLS), f32),
        in_specs=[pl.BlockSpec(memory_space=pltpu.HBM)],
        out_specs=pl.BlockSpec(memory_space=pltpu.VMEM),
        scratch_shapes=[
            pltpu.VMEM((2, NZ, BLK, NY), f32),
            pltpu.VMEM((S, 12, 72, COLS), f32),
            pltpu.VMEM((4, 48, 128), f32),
            pltpu.VMEM((4, 2, 32, COLS), f32),
            pltpu.VMEM((4, 8, 128), f32),
            pltpu.VMEM((4, 32, COLS), f32),
            pltpu.VMEM((2 * NF, 2, 80, 128), f32),
            pltpu.VMEM((2, 8 * NF, 1152), jnp.bfloat16),
            pltpu.VMEM((2, 1152, COLS), jnp.bfloat16),
            pltpu.VMEM((len(PAIRS), 8 * GROUP, 128), f32),
        ]
        + [pltpu.SemaphoreType.DMA((n,)) for n in (8, 8, 4, 4, 8, 8, 16, 16, 16, 16, 16, 4, 2)],
        name="correlate",
        compiler_params=pltpu.CompilerParams(
            collective_id=0, has_side_effects=True, vmem_limit_bytes=48 << 20
        ),
    )(pltpu.with_memory_space_constraint(x, pltpu.HBM))


def solution(mesh):
    return jax.shard_map(
        shards,
        mesh=mesh,
        in_specs=(P("sp", None, ("tx", "ty"), None),),
        out_specs=P(None, "sp", "tx", "ty"),
        check_vma=False,
    )
```

```python
import jax
import jax.numpy as jnp
from jax import lax
from jax.experimental import pallas as pl
from jax.experimental.pallas import tpu as pltpu
from jax.sharding import PartitionSpec as P

EPS = 1e-06
MESH = pl.DeviceIdType.MESH
S, NZ, NX, NY = 8, 8, 512, 1024
ROWS, COLS, BLK = 64, 256, 16
PAIRS = [(i, j) for i in range(S) for j in range(i + 1, S)]
FIELDS = [(i, None) for i in range(S)] + [(i, i) for i in range(S)] + PAIRS
NF = len(FIELDS)
Y_ORDER = ((1, 1), (3, 0), (1, 0), (3, 1))
GROUPS = (((5, 0), (6, 5), (7, 3)), ((4, 0), (5, 2), (7, 5)), ((4, 3), (5, 5), (7, 0)), ((4, 5), (6, 0), (7, 2)))
GROUP = 3
COLUMNS, CORNERS = slice(0, 32), slice(32, 48)
HALO_UNIT = 4


def kernel(
    x, o_ref, xin, m, yh, xb, yhs, xhs, yz, lhs, rhs, tmp,
    ysend, yrecv, esend, erecv, zsend, zrecv, csend, crecv, hsend, hrecv, xsend, xrecv, lsem,
):
    sp, tx, ty = (lax.axis_index(a) for a in ("sp", "tx", "ty"))
    zhi = lax.div(sp, 2)
    core = lax.rem(sp, 2)
    zsp = lax.rem(sp + 2, 4)
    csp = sp + 1 - 2 * core
    p_here = 2 * zhi
    p_there = 2 - 2 * zhi
    p_extra = 6 * zhi

    def after(k):
        return lax.rem(ty + k, 4)

    def before(k):
        return lax.rem(ty + 4 - k, 4)

    up = jnp.logical_and(ty == 3, tx < 7)
    down = jnp.logical_and(ty == 0, tx > 0)

    barrier = pltpu.get_barrier_semaphore()

    def greet(*dev):
        pl.semaphore_signal(barrier, inc=1, device_id=dev, device_id_type=MESH)

    for k in (2, 1, 3):
        greet(sp, tx, after(k))
        greet(zsp, tx, after(k))
    greet(zsp, tx, ty)
    greet(csp, tx, ty)

    @pl.when(tx > 0)
    def _():
        greet(sp, tx - 1, 3)

    @pl.when(tx < 7)
    def _():
        greet(sp, tx + 1, 0)

    load = pltpu.make_async_copy(x, xin, lsem.at[0])
    load.start()
    load.wait()
    row8 = lax.broadcasted_iota(jnp.int32, (8, 128), 0)
    lane8 = lax.broadcasted_iota(jnp.int32, (8, 128), 1)
    zero = jnp.zeros((8, 128), jnp.float32)
    for y in range(4):
        acc = zero
        for t in range(2):
            for s in range(2):
                for z in range(NZ):
                    base = 64 * t + 32 * s + 4 * z
                    at = slice(8 * t, 8 * t + 8)
                    left = xin[s, z, at, y * COLS - 128 : y * COLS] if y > 0 else zero
                    right = xin[s, z, at, y * COLS + COLS : y * COLS + COLS + 128] if y < 3 else zero
                    if y < 3:
                        right = pltpu.roll(right, base, 1) if base else right
                    if y > 0:
                        left = pltpu.roll(left, (base + 4) % 128, 1) if base != 124 else left
                    acc = jnp.where(jnp.logical_and(lane8 >= base, lane8 < base + 2), right, acc)
                    acc = jnp.where(jnp.logical_and(lane8 >= base + 2, lane8 < base + 4), left, acc)
        yhs[y] = acc

    def pack_rows(first):
        for y in range(4):
            for z in range(NZ):
                for s in range(2):
                    r = 4 * z + 2 * s
                    xhs[y, r : r + 2, :] = xin[s, z, first : first + 2, y * COLS : (y + 1) * COLS]

    for cond, first in ((up, 14), (down, 0)):

        @pl.when(cond)
        def _(first=first):
            pack_rows(first)

    pl.semaphore_wait(barrier, 8 + 4 * up.astype(jnp.int32) + 4 * down.astype(jnp.int32))

    def rcopy(src, dst, ss, rs, dev):
        return pltpu.make_async_remote_copy(
            src_ref=src, dst_ref=dst, send_sem=ss, recv_sem=rs, device_id=dev, device_id_type=MESH
        )

    def cols(y):
        return pl.ds(pl.multiple_of(y * COLS, COLS), COLS)

    def tile_of(b, t):
        return pl.ds(pl.multiple_of(b * BLK + 8 * t, 8), 8)

    def pick(u, values):
        return sum(v * (u == n).astype(jnp.int32) for n, v in enumerate(values))

    t_sent, t_got = pick(ty, (0, 0, 1)), pick(ty, (1,))
    turn = pick(ty, (1,))
    k_units = (0, 0) + (1 + 2 * turn, 3 - 2 * turn) * 2 + (2, 2)
    t_units = (0, 1, 1 - turn, turn, turn, 1 - turn, t_got, 1 - t_got)

    def eight(b):
        return pl.ds(pl.multiple_of(b * 8, 8), 8)

    zdev = (zsp, tx, ty)
    cdev = (csp, tx, ty)
    mine = pl.ds(2 * sp, 2)
    far = pl.ds(2 * zsp, 2)
    six = pl.ds(p_here + 2, 6)
    six_there = pl.ds(p_there + 2, 6)
    own_rows = pl.ds(pl.multiple_of(ty * BLK, BLK), BLK)

    def ycopy(k, t):
        return rcopy(
            x.at[:, pl.ds(p_there, 6), eight(t), cols(after(k))],
            m.at[mine, six_there, tile_of(ty, t)],
            ysend.at[2 * k + t], yrecv.at[2 * k + t], (sp, tx, after(k)),
        )

    def ecopy(k):
        return rcopy(
            x.at[:, pl.ds(p_extra, 2), :, cols(after(k))],
            m.at[mine, pl.ds(p_extra + 2, 2), own_rows],
            esend.at[k], erecv.at[k], (sp, tx, after(k)),
        )

    def zcopy(k, t, first=False):
        dst = m.at[mine, six_there, tile_of(before(k), t)]
        src = x.at[:, pl.ds(p_there, 6), 8 * t : 8 * t + 8, cols(ty)] if first else dst
        return rcopy(src, dst, zsend.at[2 * k + t], zrecv.at[2 * k + t], zdev)

    def ccopy(k, t, first=False):
        dst = m.at[mine, six, tile_of(before(k), t)]
        src = x.at[:, pl.ds(p_here, 6), 8 * t : 8 * t + 8, cols(ty)] if first else dst
        return rcopy(src, dst, csend.at[2 * k + t], crecv.at[2 * k + t], cdev)

    def cfcopy(k, t):
        ref = m.at[far, six, tile_of(before(k), t)]
        return rcopy(ref, ref, csend.at[8 + 2 * k + t], crecv.at[8 + 2 * k + t], cdev)

    def hcopy(k, there):
        dev = (zsp if there else sp, tx, after(k))
        q = 4 * there + k
        return rcopy(yhs.at[after(k)], yh.at[sp, eight(ty)], hsend.at[q], hrecv.at[q], dev)

    def xcopies(side, y):
        dev = (sp, tx + 1 if side == 0 else tx - 1, y)
        q = 2 * (4 * side + y)
        return (
            rcopy(xhs.at[y], xb.at[sp, side], xsend.at[q], xrecv.at[2 * side], dev),
            rcopy(
                yhs.at[y], yh.at[sp, 32 + 8 * side : 40 + 8 * side],
                xsend.at[q + 1], xrecv.at[2 * side + 1], dev,
            ),
        )

    def xrows(first):
        return pl.ds(pl.multiple_of(first * 4, 8), 24)

    def xz():
        ref = xb.at[sp, :, xrows(p_there)]
        return rcopy(ref, ref, hsend.at[8], hrecv.at[8], zdev)

    def yzcopy():
        ref = yh.at[sp, CORNERS]
        return rcopy(ref, ref, hsend.at[9], hrecv.at[9], zdev)

    def xc(q, who):
        ref = xb.at[who, :, xrows(p_here)]
        return rcopy(ref, ref, hsend.at[10 + q], hrecv.at[10 + q], cdev)

    def yc(q, who, part):
        ref = yh.at[who, part]
        q = q + (12 if part is COLUMNS else 14)
        return rcopy(ref, ref, hsend.at[q], hrecv.at[q], cdev)

    zcopy(0, 0, True).start()
    for side, cond, first in ((0, up, 14), (1, down, 0)):

        @pl.when(cond)
        def _(side=side, first=first):
            for y in range(4):
                for c in xcopies(side, y):
                    c.start()

    yh[sp, eight(ty)] = yhs[ty]
    for k in (2, 1, 3):
        hcopy(k, 1).start()
        hcopy(k, 0).start()
    hcopy(0, 1).start()

    for k, t in Y_ORDER[:2]:
        ycopy(k, t).start()

    zcopy(0, 1, True).start()
    for k, t in Y_ORDER[2:]:
        ycopy(k, t).start()
    for t in range(2):
        ccopy(0, t, True).start()
    own = pltpu.make_async_copy(
        x.at[:, pl.ds(p_here, 6), :, cols(ty)], m.at[mine, six, own_rows], lsem.at[1]
    )
    own.start()

    for s in range(S):
        m[s, 0:2] = jnp.zeros((2, 72, COLS), jnp.float32)
        m[s, 10:12] = jnp.zeros((2, 72, COLS), jnp.float32)

    for side, cond in ((0, tx == 0), (1, tx == 7)):

        @pl.when(cond)
        def _(side=side):
            xb[sp, side] = jnp.zeros((32, COLS), jnp.float32)
            yh[sp, 32 + 8 * side : 40 + 8 * side] = zero

    for k, t in list(zip(k_units, t_units))[2:4]:
        ycopy(k, t).wait_recv()
        zcopy(k, t).start()
    ecopy(1).start()
    ecopy(3).start()
    ycopy(2, t_sent).start()
    ycopy(2, 1 - t_sent).start()
    ecopy(2).start()

    for k in range(4):
        hcopy(k, 1).wait_recv()
        if k:
            hcopy(k, 0).wait_recv()
    yc(0, sp, COLUMNS).start()
    yc(1, zsp, COLUMNS).start()
    zcopy(0, 0).wait_recv()
    cfcopy(0, 0).start()
    for side, cond in ((0, tx > 0), (1, tx < 7)):

        @pl.when(cond)
        def _(side=side):
            for c in xcopies(side, 0):
                c.wait_recv()

    xz().start()
    yzcopy().start()
    xc(0, sp).start()
    yc(0, sp, CORNERS).start()
    for k, t in list(zip(k_units, t_units))[4:6]:
        ycopy(k, t).wait_recv()
        zcopy(k, t).start()

    r_at = lax.broadcasted_iota(jnp.int32, (COLS, COLS), 0)
    c_at = lax.broadcasted_iota(jnp.int32, (COLS, COLS), 1)
    band = jnp.where(jnp.abs(r_at - c_at) <= 2, 1.0, 0.0).astype(jnp.bfloat16)
    r_at = lax.broadcasted_iota(jnp.int32, (128, COLS), 0)
    c_at = lax.broadcasted_iota(jnp.int32, (128, COLS), 1)
    plane, kind = lax.div(r_at, 4), lax.rem(r_at, 4)
    ends = (
        ((kind == 0) & (c_at >= COLS - 2))
        | ((kind == 1) & (c_at == COLS - 1))
        | ((kind == 2) & (c_at == 0))
        | ((kind == 3) & (c_at <= 1))
    )
    for p in range(2):
        part = jnp.where(ends & (plane >= p) & (plane <= p + 4), 1.0, 0.0).astype(jnp.bfloat16)
        for q in range(3):
            rhs[p, 256 * q : 256 * q + 256, :] = band
            rhs[p, 768 + 128 * q : 896 + 128 * q, :] = part

    zcopy(0, 1).wait_recv()
    cfcopy(0, 1).start()
    own.wait()
    for q in range(2):
        yc(q, sp, COLUMNS).wait_recv()

    def split(v):
        hi = v.astype(jnp.bfloat16)
        rest = v - hi.astype(jnp.float32)
        mid = rest.astype(jnp.bfloat16)
        return hi, mid, (rest - mid.astype(jnp.float32)).astype(jnp.bfloat16)

    def halo_cols(i, rows, t):
        h = pltpu.roll(yh[i // 2, rows, :], lax.rem(264 - 64 * t - 32 * (i % 2) - 8 * sp, 128), 1)
        at = 2 * sp - 2 + lax.div(lane8, 4)
        return jnp.where((at >= 0) & (at < NZ), h, 0.0)

    def stage1(rt, h, wrap=False):
        tile = pl.ds(pl.multiple_of(rt * 8, 8), 8)
        dsts = [pl.ds(pl.multiple_of(rt * 8 + 8, 8), 8)] + [pl.ds(0, 8)] * wrap
        for ct in range(2):
            v = [[m[i, 2 * sp + k, tile, ct * 128 : ct * 128 + 128] for k in range(6)] for i in range(S)]
            for f in range(0, NF, 2):
                sums = [[], []]
                for i, j in FIELDS[f : f + 2]:
                    p = v[i] if j is None else [a * b for a, b in zip(v[i], v[j])]
                    mid = (p[1] + p[2]) + (p[3] + p[4])
                    sums[0].append(p[0] + mid)
                    sums[1].append(mid + p[5])
                for p in range(2):
                    for q, part in enumerate(split(jnp.concatenate(sums[p], 0))):
                        at = 256 * q + 128 * ct
                        lhs[p, 8 * f : 8 * f + 16, at : at + 128] = part
        for f in range(0, NF, 2):
            hv = [h[i] if j is None else h[i] * h[j] for i, j in FIELDS[f : f + 2]]
            for q, part in enumerate(split(jnp.concatenate(hv, 0))):
                for p in range(2):
                    lhs[p, 8 * f : 8 * f + 16, 768 + 128 * q : 896 + 128 * q] = part
        for p in range(2):
            r = jnp.dot(lhs[p], rhs[p], preferred_element_type=jnp.float32)
            for f in range(NF):
                for ct in range(2):
                    for dst in dsts:
                        yz[2 * f + p, ct, dst, :] = r[8 * f : 8 * f + 8, 128 * ct : 128 * ct + 128]

    def halos():
        for q in range(2):
            xc(q, sp).wait_recv()
            yc(q, sp, CORNERS).wait_recv()
        for i in range(S):
            for z in range(NZ):
                r = 4 * z + 2 * (i % 2)
                m[i, 2 + z, 64:66, :] = xb[i // 2, 1, r : r + 2, :]
                m[i, 2 + z, 70:72, :] = xb[i // 2, 0, r : r + 2, :]
        h = [
            jnp.where(row8 < 4, halo_cols(i, slice(40, 48), 0), halo_cols(i, slice(32, 40), 1)) for i in range(S)
        ]
        stage1(8, h, True)

    def span(pos, extent):
        return (jnp.minimum(pos + 2, extent - 1) - jnp.maximum(pos - 2, 0) + 1).astype(jnp.float32)

    def stage2(x0):
        start = x0 * 8
        for p in range(2):
            cz = span(2 * sp + p, NZ)
            for ct in range(2):
                cy = span(ty * COLS + ct * 128 + lane8, NY) * cz
                inv = [1.0 / (span(tx * ROWS + start + row8 * GROUP + q, NX) * cy) for q in range(GROUP)]

                def box(f):
                    w = [yz[2 * f + p, ct, pl.ds(start + 6 + q, 8, stride=GROUP), :] for q in range(GROUP + 4)]
                    a = [w[q] + w[q + 1] for q in range(GROUP + 3)]
                    return [((a[q] + a[q + 2]) + w[q + 4]) * inv[q] for q in range(GROUP)]

                means = [box(i) for i in range(S)]
                var = [[b - u * u + EPS for b, u in zip(box(S + i), means[i])] for i in range(S)]
                for n, (i, j) in enumerate(PAIRS):
                    b = box(2 * S + n)
                    for q in range(GROUP):
                        cov = b[q] - means[i][q] * means[j][q]
                        tmp[n, pl.ds(q, 8, stride=GROUP), :] = cov * lax.rsqrt(var[i][q] * var[j][q])
                for n in range(len(PAIRS)):
                    o_ref[n, p, pl.ds(pl.multiple_of(start, 8), 8 * GROUP), ct * 128 : ct * 128 + 128] = tmp[n]

    def unit(u):
        return pick(u, k_units), pick(u, t_units)

    def step(u, _):
        @pl.when(jnp.logical_and(u >= 2, u < 8))
        def _():
            k, t = unit(u)
            zcopy(k, t).wait_recv()
            cfcopy(k, t).start()

        for n, t in ((3, t_got), (4, 1 - t_got)):

            @pl.when(u == n)
            def _(t=t):
                ycopy(2, t).wait_recv()
                zcopy(2, t).start()

        for n, k in ((1, k_units[2]), (2, k_units[3]), (5, 2)):

            @pl.when(u == n)
            def _(k=k):
                ecopy(k).wait_recv()
                for t in range(2):
                    ccopy(k, t).start()

        @pl.when(u == HALO_UNIT)
        def _():
            xz().wait_recv()
            xc(1, zsp).start()
            yzcopy().wait_recv()
            yc(1, zsp, CORNERS).start()

        @pl.when(u >= 1)
        def _():
            k, t = unit(u - 1)
            b = before(k)

            ccopy(k, t).wait_recv()
            cfcopy(k, t).wait_recv()

            stage1(2 * b + t, [halo_cols(i, eight(b), t) for i in range(S)])

            @pl.when(u - 1 == HALO_UNIT)
            def _():
                halos()

            group = sum(
                (g0 + 1) * ((ty == y) & (u - 1 == n)).astype(jnp.int32) for y in range(4) for n, g0 in GROUPS[y]
            )

            @pl.when(group > 0)
            def _():
                stage2(group - 1)

        return 0

    lax.fori_loop(0, 9, step, 0)

    for k in range(4):
        for t in range(2):
            zcopy(k, t).wait_send()
            ccopy(k, t).wait_send()
            cfcopy(k, t).wait_send()
            if k:
                ycopy(k, t).wait_send()
        if k:
            ecopy(k).wait_send()
            hcopy(k, 0).wait_send()
        hcopy(k, 1).wait_send()
    xz().wait_send()
    yzcopy().wait_send()
    for q in range(2):
        for c in (xc(q, sp), yc(q, sp, COLUMNS), yc(q, sp, CORNERS)):
            c.wait_send()
    for side, cond in ((0, up), (1, down)):

        @pl.when(cond)
        def _(side=side):
            for y in range(4):
                for c in xcopies(side, y):
                    c.wait_send()


def shards(x):
    f32 = jnp.float32
    return pl.pallas_call(
        kernel,
        out_shape=jax.ShapeDtypeStruct((len(PAIRS), 2, ROWS, COLS), f32),
        in_specs=[pl.BlockSpec(memory_space=pltpu.HBM)],
        out_specs=pl.BlockSpec(memory_space=pltpu.VMEM),
        scratch_shapes=[
            pltpu.VMEM((2, NZ, BLK, NY), f32),
            pltpu.VMEM((S, 12, 72, COLS), f32),
            pltpu.VMEM((4, 48, 128), f32),
            pltpu.VMEM((4, 2, 32, COLS), f32),
            pltpu.VMEM((4, 8, 128), f32),
            pltpu.VMEM((4, 32, COLS), f32),
            pltpu.VMEM((2 * NF, 2, 80, 128), f32),
            pltpu.VMEM((2, 8 * NF, 1152), jnp.bfloat16),
            pltpu.VMEM((2, 1152, COLS), jnp.bfloat16),
            pltpu.VMEM((len(PAIRS), 8 * GROUP, 128), f32),
        ]
        + [pltpu.SemaphoreType.DMA((n,)) for n in (8, 8, 4, 4, 8, 8, 16, 16, 16, 16, 16, 4, 2)],
        name="correlate",
        compiler_params=pltpu.CompilerParams(
            collective_id=0, has_side_effects=True, vmem_limit_bytes=48 << 20
        ),
    )(pltpu.with_memory_space_constraint(x, pltpu.HBM))


def solution(mesh):
    return jax.shard_map(
        shards,
        mesh=mesh,
        in_specs=(P("sp", None, ("tx", "ty"), None),),
        out_specs=P(None, "sp", "tx", "ty"),
        check_vma=False,
    )
```

```python
import jax
import jax.numpy as jnp
from jax import lax
from jax.experimental import pallas as pl
from jax.experimental.pallas import tpu as pltpu
from jax.sharding import PartitionSpec as P

EPS = 1e-06
MESH = pl.DeviceIdType.MESH
S, NZ, NX, NY = 8, 8, 512, 1024
ROWS, COLS, BLK = 64, 256, 16
PAIRS = [(i, j) for i in range(S) for j in range(i + 1, S)]
FIELDS = [(i, None) for i in range(S)] + [(i, i) for i in range(S)] + PAIRS
NF = len(FIELDS)
Y_ORDER = ((1, 1), (3, 0), (1, 0), (3, 1))
GROUPS = (((5, 0), (6, 5), (7, 3)), ((4, 0), (5, 2), (7, 5)), ((4, 3), (5, 5), (7, 0)), ((4, 5), (6, 0), (7, 2)))
GROUP = 3
COLUMNS, CORNERS = slice(0, 32), slice(32, 48)
HALO_UNIT = 4


def kernel(
    x, o_ref, xin, m, yh, xb, yhs, xhs, yz, lhs, rhs, tmp,
    ysend, yrecv, esend, erecv, zsend, zrecv, csend, crecv, hsend, hrecv, xsend, xrecv, lsem,
):
    sp, tx, ty = (lax.axis_index(a) for a in ("sp", "tx", "ty"))
    zhi = lax.div(sp, 2)
    core = lax.rem(sp, 2)
    zsp = lax.rem(sp + 2, 4)
    csp = sp + 1 - 2 * core
    p_here = 2 * zhi
    p_there = 2 - 2 * zhi
    p_extra = 6 * zhi

    def after(k):
        return lax.rem(ty + k, 4)

    def before(k):
        return lax.rem(ty + 4 - k, 4)

    up = jnp.logical_and(ty == 3, tx < 7)
    down = jnp.logical_and(ty == 0, tx > 0)

    barrier = pltpu.get_barrier_semaphore()

    def greet(*dev):
        pl.semaphore_signal(barrier, inc=1, device_id=dev, device_id_type=MESH)

    for k in (2, 1, 3):
        greet(sp, tx, after(k))
        greet(zsp, tx, after(k))
    greet(zsp, tx, ty)
    greet(csp, tx, ty)

    @pl.when(tx > 0)
    def _():
        greet(sp, tx - 1, 3)

    @pl.when(tx < 7)
    def _():
        greet(sp, tx + 1, 0)

    load = pltpu.make_async_copy(x, xin, lsem.at[0])
    load.start()
    load.wait()
    row8 = lax.broadcasted_iota(jnp.int32, (8, 128), 0)
    lane8 = lax.broadcasted_iota(jnp.int32, (8, 128), 1)
    zero = jnp.zeros((8, 128), jnp.float32)
    for y in range(4):
        acc = zero
        for t in range(2):
            for s in range(2):
                for z in range(NZ):
                    base = 64 * t + 32 * s + 4 * z
                    at = slice(8 * t, 8 * t + 8)
                    left = xin[s, z, at, y * COLS - 128 : y * COLS] if y > 0 else zero
                    right = xin[s, z, at, y * COLS + COLS : y * COLS + COLS + 128] if y < 3 else zero
                    if y < 3:
                        right = pltpu.roll(right, base, 1) if base else right
                    if y > 0:
                        left = pltpu.roll(left, (base + 4) % 128, 1) if base != 124 else left
                    acc = jnp.where(jnp.logical_and(lane8 >= base, lane8 < base + 2), right, acc)
                    acc = jnp.where(jnp.logical_and(lane8 >= base + 2, lane8 < base + 4), left, acc)
        yhs[y] = acc

    def pack_rows(first):
        for y in range(4):
            for z in range(NZ):
                for s in range(2):
                    r = 4 * z + 2 * s
                    xhs[y, r : r + 2, :] = xin[s, z, first : first + 2, y * COLS : (y + 1) * COLS]

    for cond, first in ((up, 14), (down, 0)):

        @pl.when(cond)
        def _(first=first):
            pack_rows(first)

    pl.semaphore_wait(barrier, 8 + 4 * up.astype(jnp.int32) + 4 * down.astype(jnp.int32))

    def rcopy(src, dst, ss, rs, dev):
        return pltpu.make_async_remote_copy(
            src_ref=src, dst_ref=dst, send_sem=ss, recv_sem=rs, device_id=dev, device_id_type=MESH
        )

    def cols(y):
        return pl.ds(pl.multiple_of(y * COLS, COLS), COLS)

    def tile_of(b, t):
        return pl.ds(pl.multiple_of(b * BLK + 8 * t, 8), 8)

    def pick(u, values):
        return sum(v * (u == n).astype(jnp.int32) for n, v in enumerate(values))

    t_sent, t_got = pick(ty, (0, 0, 1)), pick(ty, (1,))
    turn = pick(ty, (1,))
    k_units = (0, 0) + (1 + 2 * turn, 3 - 2 * turn) * 2 + (2, 2)
    t_units = (0, 1, 1 - turn, turn, turn, 1 - turn, t_got, 1 - t_got)

    def eight(b):
        return pl.ds(pl.multiple_of(b * 8, 8), 8)

    zdev = (zsp, tx, ty)
    cdev = (csp, tx, ty)
    mine = pl.ds(2 * sp, 2)
    far = pl.ds(2 * zsp, 2)
    six = pl.ds(p_here + 2, 6)
    six_there = pl.ds(p_there + 2, 6)
    own_rows = pl.ds(pl.multiple_of(ty * BLK, BLK), BLK)

    def ycopy(k, t):
        return rcopy(
            x.at[:, pl.ds(p_there, 6), eight(t), cols(after(k))],
            m.at[mine, six_there, tile_of(ty, t)],
            ysend.at[2 * k + t], yrecv.at[2 * k + t], (sp, tx, after(k)),
        )

    def ecopy(k):
        return rcopy(
            x.at[:, pl.ds(p_extra, 2), :, cols(after(k))],
            m.at[mine, pl.ds(p_extra + 2, 2), own_rows],
            esend.at[k], erecv.at[k], (sp, tx, after(k)),
        )

    def zcopy(k, t, first=False):
        dst = m.at[mine, six_there, tile_of(before(k), t)]
        src = x.at[:, pl.ds(p_there, 6), 8 * t : 8 * t + 8, cols(ty)] if first else dst
        return rcopy(src, dst, zsend.at[2 * k + t], zrecv.at[2 * k + t], zdev)

    def ccopy(k, t, first=False):
        dst = m.at[mine, six, tile_of(before(k), t)]
        src = x.at[:, pl.ds(p_here, 6), 8 * t : 8 * t + 8, cols(ty)] if first else dst
        return rcopy(src, dst, csend.at[2 * k + t], crecv.at[2 * k + t], cdev)

    def cfcopy(k, t):
        ref = m.at[far, six, tile_of(before(k), t)]
        return rcopy(ref, ref, csend.at[8 + 2 * k + t], crecv.at[8 + 2 * k + t], cdev)

    def zlast(s):
        ref = m.at[2 * sp + s, six_there, tile_of(before(2), 1 - t_got)]
        return rcopy(ref, ref, zsend.at[8 + s], zrecv.at[8 + s], zdev)

    def cflast(s):
        ref = m.at[2 * zsp + s, six, tile_of(before(2), 1 - t_got)]
        return rcopy(ref, ref, csend.at[16 + s], crecv.at[16 + s], cdev)

    def hcopy(k, there):
        dev = (zsp if there else sp, tx, after(k))
        q = 4 * there + k
        return rcopy(yhs.at[after(k)], yh.at[sp, eight(ty)], hsend.at[q], hrecv.at[q], dev)

    def xcopies(side, y):
        dev = (sp, tx + 1 if side == 0 else tx - 1, y)
        q = 2 * (4 * side + y)
        return (
            rcopy(xhs.at[y], xb.at[sp, side], xsend.at[q], xrecv.at[2 * side], dev),
            rcopy(
                yhs.at[y], yh.at[sp, 32 + 8 * side : 40 + 8 * side],
                xsend.at[q + 1], xrecv.at[2 * side + 1], dev,
            ),
        )

    def xrows(first):
        return pl.ds(pl.multiple_of(first * 4, 8), 24)

    def xz():
        ref = xb.at[sp, :, xrows(p_there)]
        return rcopy(ref, ref, hsend.at[8], hrecv.at[8], zdev)

    def yzcopy():
        ref = yh.at[sp, CORNERS]
        return rcopy(ref, ref, hsend.at[9], hrecv.at[9], zdev)

    def xc(q, who):
        ref = xb.at[who, :, xrows(p_here)]
        return rcopy(ref, ref, hsend.at[10 + q], hrecv.at[10 + q], cdev)

    def yc(q, who, part):
        ref = yh.at[who, part]
        q = q + (12 if part is COLUMNS else 14)
        return rcopy(ref, ref, hsend.at[q], hrecv.at[q], cdev)

    zcopy(0, 0, True).start()
    for side, cond, first in ((0, up, 14), (1, down, 0)):

        @pl.when(cond)
        def _(side=side, first=first):
            for y in range(4):
                for c in xcopies(side, y):
                    c.start()

    yh[sp, eight(ty)] = yhs[ty]
    for k in (2, 1, 3):
        hcopy(k, 1).start()
        hcopy(k, 0).start()
    hcopy(0, 1).start()

    for k, t in Y_ORDER[:2]:
        ycopy(k, t).start()

    zcopy(0, 1, True).start()
    for k, t in Y_ORDER[2:]:
        ycopy(k, t).start()
    for t in range(2):
        ccopy(0, t, True).start()
    own = pltpu.make_async_copy(
        x.at[:, pl.ds(p_here, 6), :, cols(ty)], m.at[mine, six, own_rows], lsem.at[1]
    )
    own.start()

    for s in range(S):
        m[s, 0:2] = jnp.zeros((2, 72, COLS), jnp.float32)
        m[s, 10:12] = jnp.zeros((2, 72, COLS), jnp.float32)

    for side, cond in ((0, tx == 0), (1, tx == 7)):

        @pl.when(cond)
        def _(side=side):
            xb[sp, side] = jnp.zeros((32, COLS), jnp.float32)
            yh[sp, 32 + 8 * side : 40 + 8 * side] = zero

    for k, t in list(zip(k_units, t_units))[2:4]:
        ycopy(k, t).wait_recv()
        zcopy(k, t).start()
    ecopy(1).start()
    ecopy(3).start()
    ycopy(2, t_sent).start()
    ycopy(2, 1 - t_sent).start()
    ecopy(2).start()

    for k in range(4):
        hcopy(k, 1).wait_recv()
        if k:
            hcopy(k, 0).wait_recv()
    yc(0, sp, COLUMNS).start()
    yc(1, zsp, COLUMNS).start()
    zcopy(0, 0).wait_recv()
    cfcopy(0, 0).start()
    for side, cond in ((0, tx > 0), (1, tx < 7)):

        @pl.when(cond)
        def _(side=side):
            for c in xcopies(side, 0):
                c.wait_recv()

    xz().start()
    yzcopy().start()
    xc(0, sp).start()
    yc(0, sp, CORNERS).start()
    for k, t in list(zip(k_units, t_units))[4:6]:
        ycopy(k, t).wait_recv()
        zcopy(k, t).start()

    r_at = lax.broadcasted_iota(jnp.int32, (COLS, COLS), 0)
    c_at = lax.broadcasted_iota(jnp.int32, (COLS, COLS), 1)
    band = jnp.where(jnp.abs(r_at - c_at) <= 2, 1.0, 0.0).astype(jnp.bfloat16)
    r_at = lax.broadcasted_iota(jnp.int32, (128, COLS), 0)
    c_at = lax.broadcasted_iota(jnp.int32, (128, COLS), 1)
    plane, kind = lax.div(r_at, 4), lax.rem(r_at, 4)
    ends = (
        ((kind == 0) & (c_at >= COLS - 2))
        | ((kind == 1) & (c_at == COLS - 1))
        | ((kind == 2) & (c_at == 0))
        | ((kind == 3) & (c_at <= 1))
    )
    for p in range(2):
        part = jnp.where(ends & (plane >= p) & (plane <= p + 4), 1.0, 0.0).astype(jnp.bfloat16)
        for q in range(3):
            rhs[p, 256 * q : 256 * q + 256, :] = band
            rhs[p, 768 + 128 * q : 896 + 128 * q, :] = part

    zcopy(0, 1).wait_recv()
    cfcopy(0, 1).start()
    own.wait()
    for q in range(2):
        yc(q, sp, COLUMNS).wait_recv()

    def split(v):
        hi = v.astype(jnp.bfloat16)
        rest = v - hi.astype(jnp.float32)
        mid = rest.astype(jnp.bfloat16)
        return hi, mid, (rest - mid.astype(jnp.float32)).astype(jnp.bfloat16)

    def halo_cols(i, rows, t):
        h = pltpu.roll(yh[i // 2, rows, :], lax.rem(264 - 64 * t - 32 * (i % 2) - 8 * sp, 128), 1)
        at = 2 * sp - 2 + lax.div(lane8, 4)
        return jnp.where((at >= 0) & (at < NZ), h, 0.0)

    def stage1(rt, h, wrap=False):
        tile = pl.ds(pl.multiple_of(rt * 8, 8), 8)
        dsts = [pl.ds(pl.multiple_of(rt * 8 + 8, 8), 8)] + [pl.ds(0, 8)] * wrap
        for ct in range(2):
            v = [[m[i, 2 * sp + k, tile, ct * 128 : ct * 128 + 128] for k in range(6)] for i in range(S)]
            for f in range(0, NF, 2):
                sums = [[], []]
                for i, j in FIELDS[f : f + 2]:
                    p = v[i] if j is None else [a * b for a, b in zip(v[i], v[j])]
                    mid = (p[1] + p[2]) + (p[3] + p[4])
                    sums[0].append(p[0] + mid)
                    sums[1].append(mid + p[5])
                for p in range(2):
                    for q, part in enumerate(split(jnp.concatenate(sums[p], 0))):
                        at = 256 * q + 128 * ct
                        lhs[p, 8 * f : 8 * f + 16, at : at + 128] = part
        for f in range(0, NF, 2):
            hv = [h[i] if j is None else h[i] * h[j] for i, j in FIELDS[f : f + 2]]
            for q, part in enumerate(split(jnp.concatenate(hv, 0))):
                for p in range(2):
                    lhs[p, 8 * f : 8 * f + 16, 768 + 128 * q : 896 + 128 * q] = part
        for p in range(2):
            r = jnp.dot(lhs[p], rhs[p], preferred_element_type=jnp.float32)
            for f in range(NF):
                for ct in range(2):
                    for dst in dsts:
                        yz[2 * f + p, ct, dst, :] = r[8 * f : 8 * f + 8, 128 * ct : 128 * ct + 128]

    def halos():
        for q in range(2):
            xc(q, sp).wait_recv()
            yc(q, sp, CORNERS).wait_recv()
        for i in range(S):
            for z in range(NZ):
                r = 4 * z + 2 * (i % 2)
                m[i, 2 + z, 64:66, :] = xb[i // 2, 1, r : r + 2, :]
                m[i, 2 + z, 70:72, :] = xb[i // 2, 0, r : r + 2, :]
        h = [
            jnp.where(row8 < 4, halo_cols(i, slice(40, 48), 0), halo_cols(i, slice(32, 40), 1)) for i in range(S)
        ]
        stage1(8, h, True)

    def span(pos, extent):
        return (jnp.minimum(pos + 2, extent - 1) - jnp.maximum(pos - 2, 0) + 1).astype(jnp.float32)

    def stage2(x0):
        start = x0 * 8
        for p in range(2):
            cz = span(2 * sp + p, NZ)
            for ct in range(2):
                cy = span(ty * COLS + ct * 128 + lane8, NY) * cz
                inv = [1.0 / (span(tx * ROWS + start + row8 * GROUP + q, NX) * cy) for q in range(GROUP)]

                def box(f):
                    w = [yz[2 * f + p, ct, pl.ds(start + 6 + q, 8, stride=GROUP), :] for q in range(GROUP + 4)]
                    a = [w[q] + w[q + 1] for q in range(GROUP + 3)]
                    return [((a[q] + a[q + 2]) + w[q + 4]) * inv[q] for q in range(GROUP)]

                means = [box(i) for i in range(S)]
                var = [[b - u * u + EPS for b, u in zip(box(S + i), means[i])] for i in range(S)]
                for n, (i, j) in enumerate(PAIRS):
                    b = box(2 * S + n)
                    for q in range(GROUP):
                        cov = b[q] - means[i][q] * means[j][q]
                        tmp[n, pl.ds(q, 8, stride=GROUP), :] = cov * lax.rsqrt(var[i][q] * var[j][q])
                for n in range(len(PAIRS)):
                    o_ref[n, p, pl.ds(pl.multiple_of(start, 8), 8 * GROUP), ct * 128 : ct * 128 + 128] = tmp[n]

    def unit(u):
        return pick(u, k_units), pick(u, t_units)

    def step(u, _):
        @pl.when(jnp.logical_and(u >= 2, u < 7))
        def _():
            k, t = unit(u)
            zcopy(k, t).wait_recv()
            cfcopy(k, t).start()

        @pl.when(u == 7)
        def _():
            for s in range(2):
                zlast(s).wait_recv()
                cflast(s).start()

        @pl.when(u == 3)
        def _():
            ycopy(2, t_got).wait_recv()
            zcopy(2, t_got).start()

        @pl.when(u == 4)
        def _():
            ycopy(2, 1 - t_got).wait_recv()
            for s in range(2):
                zlast(s).start()

        for n, k in ((1, k_units[2]), (2, k_units[3]), (5, 2)):

            @pl.when(u == n)
            def _(k=k):
                ecopy(k).wait_recv()
                for t in range(2):
                    ccopy(k, t).start()

        @pl.when(u == HALO_UNIT)
        def _():
            xz().wait_recv()
            xc(1, zsp).start()
            yzcopy().wait_recv()
            yc(1, zsp, CORNERS).start()

        @pl.when(u >= 1)
        def _():
            k, t = unit(u - 1)
            b = before(k)

            ccopy(k, t).wait_recv()

            @pl.when(u < 8)
            def _():
                cfcopy(k, t).wait_recv()

            @pl.when(u == 8)
            def _():
                for s in range(2):
                    cflast(s).wait_recv()

            stage1(2 * b + t, [halo_cols(i, eight(b), t) for i in range(S)])

            @pl.when(u - 1 == HALO_UNIT)
            def _():
                halos()

            group = sum(
                (g0 + 1) * ((ty == y) & (u - 1 == n)).astype(jnp.int32) for y in range(4) for n, g0 in GROUPS[y]
            )

            @pl.when(group > 0)
            def _():
                stage2(group - 1)

        return 0

    lax.fori_loop(0, 9, step, 0)

    for k in range(4):
        for t in range(2):
            if k != 2:
                zcopy(k, t).wait_send()
                cfcopy(k, t).wait_send()
            ccopy(k, t).wait_send()
            if k:
                ycopy(k, t).wait_send()
        if k:
            ecopy(k).wait_send()
            hcopy(k, 0).wait_send()
        hcopy(k, 1).wait_send()
    zcopy(2, t_got).wait_send()
    cfcopy(2, t_got).wait_send()
    for s in range(2):
        zlast(s).wait_send()
        cflast(s).wait_send()
    xz().wait_send()
    yzcopy().wait_send()
    for q in range(2):
        for c in (xc(q, sp), yc(q, sp, COLUMNS), yc(q, sp, CORNERS)):
            c.wait_send()
    for side, cond in ((0, up), (1, down)):

        @pl.when(cond)
        def _(side=side):
            for y in range(4):
                for c in xcopies(side, y):
                    c.wait_send()


def shards(x):
    f32 = jnp.float32
    return pl.pallas_call(
        kernel,
        out_shape=jax.ShapeDtypeStruct((len(PAIRS), 2, ROWS, COLS), f32),
        in_specs=[pl.BlockSpec(memory_space=pltpu.HBM)],
        out_specs=pl.BlockSpec(memory_space=pltpu.VMEM),
        scratch_shapes=[
            pltpu.VMEM((2, NZ, BLK, NY), f32),
            pltpu.VMEM((S, 12, 72, COLS), f32),
            pltpu.VMEM((4, 48, 128), f32),
            pltpu.VMEM((4, 2, 32, COLS), f32),
            pltpu.VMEM((4, 8, 128), f32),
            pltpu.VMEM((4, 32, COLS), f32),
            pltpu.VMEM((2 * NF, 2, 80, 128), f32),
            pltpu.VMEM((2, 8 * NF, 1152), jnp.bfloat16),
            pltpu.VMEM((2, 1152, COLS), jnp.bfloat16),
            pltpu.VMEM((len(PAIRS), 8 * GROUP, 128), f32),
        ]
        + [pltpu.SemaphoreType.DMA((n,)) for n in (8, 8, 4, 4, 10, 10, 18, 18, 16, 16, 16, 4, 2)],
        name="correlate",
        compiler_params=pltpu.CompilerParams(
            collective_id=0, has_side_effects=True, vmem_limit_bytes=48 << 20
        ),
    )(pltpu.with_memory_space_constraint(x, pltpu.HBM))


def solution(mesh):
    return jax.shard_map(
        shards,
        mesh=mesh,
        in_specs=(P("sp", None, ("tx", "ty"), None),),
        out_specs=P(None, "sp", "tx", "ty"),
        check_vma=False,
    )
```
